1024 devices in a mesh: samp: 8 (over x), proto: 128 (over y, z, core).
Axes of the slice: x: 8, y: 8, z: 8, core: 2. Of those that a mesh axis runs over, the one named last changes fastest.
Arguments:
- embeddings: bfloat16 [2, 4096, 256], P(None, 'samp'), may hold values from -60 to 60
- prototypes: bfloat16 [65536, 256], P('proto'), may hold values from -12 to 12
Outputs:
- grad_embed: bfloat16 [2, 4096, 256], P(None, 'samp')
- grad_proto: bfloat16 [65536, 256], P('proto')
- loss: float32 [2, 4096], P(None, 'samp')
The draws below stay inside these ranges and needn't reach their ends.
All inputs are finite; a program needn't handle non-finite values.
Results may differ from the reference program's by a relative error of at most 0.001.
The reference program's roundings to bfloat16 on the way count: a program that leaves them out, or rounds other values in their place, can miss the bound.
Values may be sent and summed in bfloat16 or wider, within the bound.
A program may use at most 32 MiB of HBM per device.

```python
import math
import jax
import jax.numpy as jnp
from jax import lax

D = 256
ITERS = 3
PROTOS = 65536
SAMPLES = 4096


cluster_count = 8


noise_spread = 0.6


def shared_centers(key, alpha_lo, alpha_hi):
    common = jnp.clip(jax.random.normal(jax.random.fold_in(key, 11), (D,), jnp.float32), -4.0, 4.0)
    own_rows = jnp.clip(jax.random.normal(jax.random.fold_in(key, 12), (cluster_count, D), jnp.float32), -4.0, 4.0)
    alpha = jax.random.uniform(jax.random.fold_in(key, 13), (cluster_count, 1), jnp.float32, alpha_lo, alpha_hi)
    return alpha * common[None, :] + own_rows


def sorted_labels(key, count):
    cluster_weights = jax.random.randint(jax.random.fold_in(key, 1), (cluster_count,), 1, 17, jnp.int32)
    bounds = jnp.cumsum(cluster_weights).astype(jnp.int32)
    picks = jax.random.randint(jax.random.fold_in(key, 2), (count,), 0, bounds[-1], jnp.int32)
    labels = jnp.sum((picks[:, None] >= bounds[None, :-1]).astype(jnp.int32), axis=1)
    return jnp.sort(labels).astype(jnp.int32)


def draw_prototypes(key, part):
    centers = shared_centers(key, 1.2, 2.0)
    key = jax.random.fold_in(key, 101)
    labels = sorted_labels(jax.random.fold_in(key, 5), PROTOS)
    own_part = noise_spread * jnp.clip(jax.random.normal(jax.random.fold_in(key, 23), (PROTOS, D), jnp.float32), -4.0, 4.0)
    summed = jnp.take(centers, labels, axis=0) + own_part
    return jnp.clip(summed, -12.0, 12.0).astype(jnp.bfloat16)


def draw_embeddings(key, part):
    centers = shared_centers(key, 1.2, 2.0)
    key = jax.random.fold_in(key, 202)
    labels = sorted_labels(jax.random.fold_in(key, 6), SAMPLES)
    own_part = noise_spread * jnp.clip(jax.random.normal(jax.random.fold_in(key, 23), (2, SAMPLES, D), jnp.float32), -4.0, 4.0)
    row_scale = jnp.exp(jax.random.uniform(jax.random.fold_in(key, 32), (2, SAMPLES, 1), jnp.float32, 0.0, math.log(10.0)))
    summed = jnp.take(centers, labels, axis=0)[None, :, :] + own_part
    return jnp.clip(summed * row_scale, -60.0, 60.0).astype(jnp.bfloat16)


def setup_inputs(seed: int = 0) -> dict:
    key_list = jax.random.split(jax.random.key(seed), 3)
    return {
        "embeddings": draw_embeddings(jax.random.fold_in(key_list[2], 71), 0),
        "prototypes": draw_prototypes(jax.random.fold_in(key_list[2], 71), 0),
    }


EPS_SINK = 0.05
TEMPER = 0.1

def normalize_rows(values):
    as_float = values.astype(jnp.float32)
    inverse = lax.rsqrt(lax.optimization_barrier(jnp.sum(as_float * as_float, axis=-1, keepdims=True)) + 1e-06)
    return (as_float * inverse, inverse)

def project(summed, unit_rows, inverse):
    return (summed - unit_rows * lax.optimization_barrier(jnp.sum(unit_rows * summed, axis=-1, keepdims=True))) * inverse

def reference(embeddings, prototypes):
    unit_emb, inverse_emb = normalize_rows(embeddings)
    unit_proto, inverse_proto = normalize_rows(prototypes)
    emb_wide = lax.optimization_barrier(unit_emb.astype(jnp.bfloat16)).astype(jnp.float32)
    proto_wide = lax.optimization_barrier(unit_proto.astype(jnp.bfloat16)).astype(jnp.float32)
    block_size = math.gcd(PROTOS, 512)
    num_blocks = PROTOS // block_size
    proto_blocks = proto_wide.reshape(num_blocks, block_size, D)

    def block_scores(proto_blk):
        return jnp.einsum('vbd,kd->vbk', emb_wide, proto_blk)
    weights = jnp.ones((2, SAMPLES), jnp.float32)
    scale_blocks = jnp.ones((num_blocks, 2, block_size), jnp.float32)
    for sweep in range(ITERS):

        def column_sums(proto_blk, weights=weights):
            sink_exp = jnp.exp(block_scores(proto_blk) / EPS_SINK)
            return 1.0 / lax.optimization_barrier(jnp.sum(sink_exp * weights[:, :, None], axis=1))
        scale_blocks = lax.map(column_sums, proto_blocks)

        def row_part(running, inputs):
            proto_blk, scale_blk = inputs
            sink_exp = jnp.exp(block_scores(proto_blk) / EPS_SINK)
            return (running + lax.optimization_barrier(jnp.sum(sink_exp * scale_blk[:, None, :], axis=2)), None)
        totals, ignored = lax.scan(row_part, jnp.zeros((2, SAMPLES), jnp.float32), (proto_blocks, scale_blocks))
        weights = 1.0 / totals

    def assignment(scores, scale_blk):
        return jnp.exp(scores / EPS_SINK) * scale_blk[:, None, :] * weights[:, :, None]

    def final_pass(running, inputs):
        proto_blk, scale_blk = inputs
        scores = block_scores(proto_blk)
        swapped = assignment(scores, scale_blk)[::-1]
        soft_sum = lax.optimization_barrier(jnp.sum(jnp.exp(scores / TEMPER), axis=2))
        cross_sum = lax.optimization_barrier(jnp.sum(swapped * scores, axis=2))
        mass_sum = lax.optimization_barrier(jnp.sum(swapped, axis=2))
        return ((running[0] + soft_sum, running[1] + cross_sum, running[2] + mass_sum), None)
    zeros_rows = jnp.zeros((2, SAMPLES), jnp.float32)
    sums_out, ignored = lax.scan(final_pass, (zeros_rows, zeros_rows, zeros_rows), (proto_blocks, scale_blocks))
    soft_total, cross_total, mass_total = sums_out
    loss = jnp.log(soft_total) * mass_total - cross_total / TEMPER

    def grad_pass(running, inputs):
        proto_blk, scale_blk = inputs
        scores = block_scores(proto_blk)
        swapped = assignment(scores, scale_blk)[::-1]
        softmax_p = jnp.exp(scores / TEMPER) / soft_total[:, :, None]
        slope_bf = ((softmax_p - swapped) / TEMPER).astype(jnp.bfloat16)
        slope_wide = lax.optimization_barrier(slope_bf).astype(jnp.float32)
        running = running + jnp.einsum('vbk,kd->vbd', slope_wide, proto_blk)
        proto_part = jnp.einsum('vbk,vbd->kd', slope_wide, emb_wide)
        return (running, proto_part)
    emb_grad, proto_parts = lax.scan(grad_pass, jnp.zeros((2, SAMPLES, D), jnp.float32), (proto_blocks, scale_blocks))
    proto_grad = proto_parts.reshape(PROTOS, D)
    grad_embed = project(emb_grad, unit_emb, inverse_emb).astype(jnp.bfloat16)
    grad_proto = project(proto_grad, unit_proto, inverse_proto).astype(jnp.bfloat16)
    return (grad_embed, grad_proto, loss)
```

```python
import functools

import jax
import jax.numpy as jnp
from jax import lax
from jax.experimental import pallas as pl
from jax.experimental.pallas import tpu as pltpu
from jax.sharding import PartitionSpec as P

ITERS = 3
INV_TEMPER = 10.0
F32 = jnp.float32
BF16 = jnp.bfloat16
MESH = pl.DeviceIdType.MESH
LANES = 128


def normalize_rows(values):
    as_float = values.astype(F32)
    inverse = lax.rsqrt(jnp.sum(as_float * as_float, axis=-1, keepdims=True) + 1e-06)
    return as_float * inverse, inverse


def project(summed, unit_rows, inverse):
    return (summed - unit_rows * jnp.sum(unit_rows * summed, axis=-1, keepdims=True)) * inverse


def far_first(count):
    half = count // 2
    order = [half]
    for step in range(1, half + 1):
        for offset in (half - step, half + step):
            if 0 < offset < count and offset not in order:
                order.append(offset)
    return order


def kernel(
    nx,
    ny,
    emb_ref,
    proto_ref,
    ge_ref,
    gp_ref,
    loss_ref,
    eb_ref,
    pb_ref,
    s_ref,
    soft_ref,
    sink_ref,
    slope_ref,
    epart_ref,
    ppart_ref,
    wcol_ref,
    tcol_ref,
    col_buf,
    row_buf,
    rowz_buf,
    sib_buf,
    a_buf,
    b_buf,
    x_buf,
    send_sem,
    recv_sem,
):
    rows, width = eb_ref.shape
    half = rows // 2
    cols = pb_ref.shape[0]
    x = lax.axis_index("samp")
    p = lax.axis_index("proto")
    y = p // (2 * ny)
    z = (p // 2) % ny
    c = p % 2
    pos = y * 2 + c
    ai = y + (z - y) * c
    bi = z + (y - z) * c
    astep = 2 * ny + (2 - 2 * ny) * c
    bstep = 2 + (2 * ny - 2) * c
    ablock = rows // 2 // ny
    xblock = cols // nx

    def at_x(j):
        return (j, p)

    def at_yc(j):
        return (x, (j // 2) * (2 * ny) + z * 2 + j % 2)

    def at_z(j):
        return (x, y * (2 * ny) + j * 2 + c)

    def at_a(j):
        return (x, p + (j - ai) * astep)

    def at_b(j):
        return (x, p + (j - bi) * bstep)

    def at_ac(j):
        return (x, p + (j // 2 - ai) * astep + j % 2 - c)

    sibling = (x, p + 1 - 2 * c)

    barrier = pltpu.get_barrier_semaphore()

    def greet(device):
        pl.semaphore_signal(barrier, inc=1, device_id=device, device_id_type=MESH)

    for d in range(1, nx):
        greet(at_x(lax.rem(x + d, nx)))
    for d in range(1, ny):
        for core in range(2):
            greet((x, lax.rem(y + d, ny) * (2 * ny) + z * 2 + core))
            greet((x, y * (2 * ny) + lax.rem(z + d, ny) * 2 + core))
    greet(sibling)

    pending = []

    def flush():
        for copy in pending:
            copy.wait_send()
        pending.clear()

    def start(stage, count, me, at, source, place):
        for d in far_first(count):
            j = lax.rem(me + d, count)
            copy = pltpu.make_async_remote_copy(
                src_ref=source(j),
                dst_ref=place(me),
                send_sem=send_sem.at[stage, d],
                recv_sem=recv_sem.at[stage, me],
                device_id=at(j),
                device_id_type=MESH,
            )
            copy.start()
            pending.append(copy)

    def wait(stage, count, me, at, place):
        for d in range(1, count):
            j = lax.rem(me + d, count)
            pltpu.make_async_remote_copy(
                src_ref=place(j),
                dst_ref=place(j),
                send_sem=send_sem.at[stage, d],
                recv_sem=recv_sem.at[stage, j],
                device_id=at(j),
                device_id_type=MESH,
            ).wait_recv()

    def total_of(ref, count):
        total = ref[0]
        for j in range(1, count):
            total = total + ref[j]
        return total

    def wide(column):
        return jnp.concatenate([column] * (cols // LANES), axis=1)

    def narrow(block):
        total = block[:, :LANES]
        for j in range(1, cols // LANES):
            total = total + block[:, j * LANES : (j + 1) * LANES]
        return jnp.sum(total.T, axis=0, keepdims=True)

    step = min(256, half)
    blocks = [(v, i) for v in range(2) for i in range(v * half, (v + 1) * half, step)]

    unit_proto, _ = normalize_rows(proto_ref[...])
    pb_ref[...] = unit_proto.astype(BF16)
    sums = [None, None]
    for v, i in blocks:
        unit, _ = normalize_rows(emb_ref[i : i + step, :])
        eb = unit.astype(BF16)
        eb_ref[i : i + step, :] = eb
        s = lax.dot_general(eb, pb_ref[...], (((1,), (1,)), ((), ())), preferred_element_type=F32)
        s_ref[i : i + step, :] = s
        soft = jnp.exp(s * INV_TEMPER)
        soft_ref[i : i + step, :] = soft
        sink = soft * soft
        sink_ref[i : i + step, :] = sink
        part = jnp.sum(sink, axis=0, keepdims=True)
        sums[v] = part if sums[v] is None else sums[v] + part

    def store_columns(ref, row):
        for i in range(0, rows, step):
            ref[i : i + step, :] = jnp.broadcast_to(row[:, i : i + step], (LANES, step)).T

    pl.semaphore_wait(barrier, nx - 1 + 4 * (ny - 1) + 1)

    soft_total = None
    weights = None
    scale = None
    SOFT_YC, SOFT_Z = 3, 3
    for sweep in range(ITERS):
        if sweep > 0:
            sums = [None, None]
            for v, i in blocks:
                part = jnp.sum(sink_ref[i : i + step, :] * wide(wcol_ref[i : i + step, :]), axis=0, keepdims=True)
                sums[v] = part if sums[v] is None else sums[v] + part
        stage = 3 * sweep
        col = col_buf.at[sweep]
        for v in range(2):
            col[x, v : v + 1, :] = sums[v]
        start(stage, nx, x, at_x, lambda j: col.at[x], lambda j: col.at[j])
        if sweep == 0:
            for v, i in blocks:
                row_buf[SOFT_YC, pos, :, i : i + step] = narrow(soft_ref[i : i + step, :])
            extra = row_buf.at[SOFT_YC]
            start(9, 2 * ny, pos, at_yc, lambda j: extra.at[pos], lambda j: extra.at[j])
        wait(stage, nx, x, at_x, lambda j: col.at[j])
        scale = 1.0 / total_of(col, nx)
        row = row_buf.at[sweep]
        for v, i in blocks:
            row[pos, :, i : i + step] = narrow(sink_ref[i : i + step, :] * scale[v : v + 1, :])
        start(stage + 1, 2 * ny, pos, at_yc, lambda j: row.at[pos], lambda j: row.at[j])
        if sweep == 0:
            wait(9, 2 * ny, pos, at_yc, lambda j: extra.at[j])
            extraz = rowz_buf.at[SOFT_Z]
            extraz[z] = total_of(extra, 2 * ny)
            start(10, ny, z, at_z, lambda j: extraz.at[z], lambda j: extraz.at[j])
        wait(stage + 1, 2 * ny, pos, at_yc, lambda j: row.at[j])
        rowz = rowz_buf.at[sweep]
        rowz[z] = total_of(row, 2 * ny)
        start(stage + 2, ny, z, at_z, lambda j: rowz.at[z], lambda j: rowz.at[j])
        if sweep == 1:
            wait(10, ny, z, at_z, lambda j: extraz.at[j])
            soft_total = total_of(extraz, ny)
            store_columns(tcol_ref, INV_TEMPER / soft_total)
        flush()
        wait(stage + 2, ny, z, at_z, lambda j: rowz.at[j])
        weights = 1.0 / total_of(rowz, ny)
        store_columns(wcol_ref, weights)

    scaled = scale * INV_TEMPER
    for v, i in blocks:
        o = i + half * (1 - 2 * v)
        pull = sink_ref[o : o + step, :] * scaled[1 - v : 2 - v, :] * wide(wcol_ref[o : o + step, :])
        push = soft_ref[i : i + step, :] * wide(tcol_ref[i : i + step, :])
        slope = (push - pull).astype(BF16)
        slope_ref[i : i + step, :] = slope
        epart_ref[v, i - v * half : i - v * half + step, :] = jnp.dot(
            slope, pb_ref[...], preferred_element_type=F32
        )
    to_sibling = pltpu.make_async_remote_copy(
        src_ref=epart_ref.at[1 - c],
        dst_ref=sib_buf,
        send_sem=send_sem.at[11, 0],
        recv_sem=recv_sem.at[11, 0],
        device_id=sibling,
        device_id_type=MESH,
    )
    to_sibling.start()
    for k in range(0, cols, LANES):
        ppart_ref[k : k + LANES, :] = lax.dot_general(
            slope_ref[:, k : k + LANES], eb_ref[...], (((0,), (0,)), ((), ())), preferred_element_type=F32
        )
    start(12, nx, x, at_x, lambda j: ppart_ref.at[pl.ds(j * xblock, xblock)], lambda j: x_buf.at[j])
    x_buf[x] = ppart_ref[pl.ds(x * xblock, xblock), :]

    to_sibling.wait_recv()
    for i in range(0, half, step):
        sib_buf[i : i + step, :] = sib_buf[i : i + step, :] + epart_ref[c, i : i + step, :]
    start(13, ny, ai, at_a, lambda j: sib_buf.at[pl.ds(j * ablock, ablock)], lambda j: a_buf.at[j])
    a_buf[ai] = sib_buf[pl.ds(ai * ablock, ablock), :]

    CROSS_YC, CROSS_Z = 4, 4
    cross = row_buf.at[CROSS_YC]
    for v, i in blocks:
        o = i + half * (1 - 2 * v)
        cross[pos, :, i : i + step] = narrow(
            sink_ref[o : o + step, :] * scale[1 - v : 2 - v, :] * s_ref[i : i + step, :]
        )
    start(14, 2 * ny, pos, at_yc, lambda j: cross.at[pos], lambda j: cross.at[j])

    wait(13, ny, ai, at_a, lambda j: a_buf.at[j])
    b_buf[bi] = total_of(a_buf, ny)
    start(15, ny, bi, at_b, lambda j: b_buf.at[bi], lambda j: b_buf.at[j])

    wait(14, 2 * ny, pos, at_yc, lambda j: cross.at[j])
    crossz = rowz_buf.at[CROSS_Z]
    crossz[z] = total_of(cross, 2 * ny)
    start(16, ny, z, at_z, lambda j: crossz.at[z], lambda j: crossz.at[j])

    wait(12, nx, x, at_x, lambda j: x_buf.at[j])
    unit, inverse = normalize_rows(proto_ref[pl.ds(x * xblock, xblock), :])
    gp_ref[pl.ds(x * xblock, xblock), :] = project(total_of(x_buf, nx), unit, inverse).astype(BF16)
    start(
        17,
        nx,
        x,
        at_x,
        lambda j: gp_ref.at[pl.ds(x * xblock, xblock)],
        lambda j: gp_ref.at[pl.ds(j * xblock, xblock)],
    )

    base = c * half + ai * ablock
    unit, inverse = normalize_rows(emb_ref[pl.ds(base, ablock), :])
    wait(15, ny, bi, at_b, lambda j: b_buf.at[j])
    ge_ref[pl.ds(base, ablock), :] = project(total_of(b_buf, ny), unit, inverse).astype(BF16)

    def ge_place(j):
        return ge_ref.at[pl.ds((j % 2) * half + (j // 2) * ablock, ablock)]

    mine = ge_ref.at[pl.ds(base, ablock)]
    for d in far_first(ny):
        j = lax.rem(ai + d, ny)
        for other in range(2):
            copy = pltpu.make_async_remote_copy(
                src_ref=mine,
                dst_ref=mine,
                send_sem=send_sem.at[18 + other, d],
                recv_sem=recv_sem.at[18 + other, ai],
                device_id=(x, p + (j - ai) * astep + other * (1 - 2 * c)),
                device_id_type=MESH,
            )
            copy.start()
            pending.append(copy)
    across = pltpu.make_async_remote_copy(
        src_ref=mine,
        dst_ref=mine,
        send_sem=send_sem.at[19, 0],
        recv_sem=recv_sem.at[19, ai],
        device_id=sibling,
        device_id_type=MESH,
    )
    across.start()
    pending.append(across)

    wait(16, ny, z, at_z, lambda j: crossz.at[j])
    cross_total = total_of(crossz, ny)
    swapped = jnp.concatenate([weights[:, half:], weights[:, :half]], axis=1)
    loss = jnp.log(soft_total) - cross_total * swapped * INV_TEMPER
    loss_ref[0:1, :] = loss[:, :half]
    loss_ref[1:2, :] = loss[:, half:]
    to_sibling.wait_send()
    flush()
    wait(17, nx, x, at_x, lambda j: gp_ref.at[pl.ds(j * xblock, xblock)])
    for d in range(1, ny):
        j = lax.rem(ai + d, ny)
        place = ge_ref.at[pl.ds(c * half + j * ablock, ablock)]
        pltpu.make_async_remote_copy(
            src_ref=place,
            dst_ref=place,
            send_sem=send_sem.at[18, d],
            recv_sem=recv_sem.at[18, j],
            device_id=at_a(j),
            device_id_type=MESH,
        ).wait_recv()
    for j in range(ny):
        place = ge_ref.at[pl.ds((1 - c) * half + j * ablock, ablock)]
        pltpu.make_async_remote_copy(
            src_ref=place,
            dst_ref=place,
            send_sem=send_sem.at[19, 0],
            recv_sem=recv_sem.at[19, j],
            device_id=sibling,
            device_id_type=MESH,
        ).wait_recv()


def body(nx, ny, embeddings, prototypes):
    views, samples, width = embeddings.shape
    rows, cols = views * samples, prototypes.shape[0]
    ablock, xblock = samples // ny, cols // nx
    vmem = pl.BlockSpec(memory_space=pltpu.VMEM)
    ge, gp, loss = pl.pallas_call(
        functools.partial(kernel, nx, ny),
        out_shape=(
            jax.ShapeDtypeStruct((rows, width), BF16),
            jax.ShapeDtypeStruct((cols, width), BF16),
            jax.ShapeDtypeStruct((views, samples), F32),
        ),
        in_specs=[vmem, vmem],
        out_specs=(vmem, vmem, vmem),
        scratch_shapes=[
            pltpu.VMEM((rows, width), BF16),
            pltpu.VMEM((cols, width), BF16),
            pltpu.VMEM((rows, cols), F32),
            pltpu.VMEM((rows, cols), F32),
            pltpu.VMEM((rows, cols), F32),
            pltpu.VMEM((rows, cols), BF16),
            pltpu.VMEM((views, samples, width), F32),
            pltpu.VMEM((cols, width), F32),
            pltpu.VMEM((rows, LANES), F32),
            pltpu.VMEM((rows, LANES), F32),
            pltpu.VMEM((ITERS, nx, views, cols), F32),
            pltpu.VMEM((5, 2 * ny, 1, rows), F32),
            pltpu.VMEM((5, ny, 1, rows), F32),
            pltpu.VMEM((samples, width), F32),
            pltpu.VMEM((ny, ablock, width), F32),
            pltpu.VMEM((ny, ablock, width), F32),
            pltpu.VMEM((nx, xblock, width), F32),
            pltpu.SemaphoreType.DMA((20, 16)),
            pltpu.SemaphoreType.DMA((20, 16)),
        ],
        compiler_params=pltpu.CompilerParams(
            collective_id=0, has_side_effects=True, vmem_limit_bytes=48 * 2**20
        ),
    )(embeddings.reshape(rows, width), prototypes)
    return ge.reshape(views, samples, width), gp, loss


def solution(mesh):
    nx = mesh.shape["samp"]
    ny = 1
    while 2 * ny * ny < mesh.shape["proto"]:
        ny += 1
    return jax.shard_map(
        functools.partial(body, nx, ny),
        mesh=mesh,
        in_specs=(P(None, "samp", None), P("proto", None)),
        out_specs=(P(None, "samp", None), P("proto", None), P(None, "samp")),
        check_vma=False,
    )
```

```python
import functools

import jax
import jax.numpy as jnp
from jax import lax
from jax.experimental import pallas as pl
from jax.experimental.pallas import tpu as pltpu
from jax.sharding import PartitionSpec as P

ITERS = 3
INV_TEMPER = 10.0
F32 = jnp.float32
BF16 = jnp.bfloat16
MESH = pl.DeviceIdType.MESH
LANES = 128
SUB = 8


def normalize_rows(values):
    as_float = values.astype(F32)
    inverse = lax.rsqrt(jnp.sum(as_float * as_float, axis=-1, keepdims=True) + 1e-06)
    return as_float * inverse, inverse


def project(summed, unit_rows, inverse):
    return (summed - unit_rows * jnp.sum(unit_rows * summed, axis=-1, keepdims=True)) * inverse


def far_first(count):
    half = count // 2
    order = [half]
    for step in range(1, half + 1):
        for offset in (half - step, half + step):
            if 0 < offset < count and offset not in order:
                order.append(offset)
    return order


def kernel(
    nx,
    ny,
    emb_hbm,
    proto_hbm,
    ge_ref,
    gp_ref,
    loss_ref,
    emb_ref,
    proto_ref,
    eb_ref,
    pb_ref,
    soft_ref,
    sink_ref,
    slope_ref,
    epart_ref,
    ppart_ref,
    wcol_ref,
    tcol_ref,
    scale_ref,
    col_buf,
    row_buf,
    rowz_buf,
    sib_buf,
    a_buf,
    b_buf,
    x_buf,
    load_sem,
    send_sem,
    recv_sem,
    ring_sem,
):
    rows, width = eb_ref.shape
    half = rows // 2
    cols = pb_ref.shape[0]
    tiles = cols // LANES
    x = lax.axis_index("samp")
    p = lax.axis_index("proto")
    y = p // (2 * ny)
    z = (p // 2) % ny
    c = p % 2
    pos = y * 2 + c
    ai = y + (z - y) * c
    bi = z + (y - z) * c
    astep = 2 * ny + (2 - 2 * ny) * c
    bstep = 2 + (2 * ny - 2) * c
    ablock = half // ny
    xblock = cols // nx

    def at_x(j):
        return (j, p)

    def at_yc(j):
        return (x, (j // 2) * (2 * ny) + z * 2 + j % 2)

    def at_z(j):
        return (x, y * (2 * ny) + j * 2 + c)

    def at_a(j):
        return (x, p + (j - ai) * astep)

    def at_b(j):
        return (x, p + (j - bi) * bstep)

    sibling = (x, p + 1 - 2 * c)

    load_proto = pltpu.make_async_copy(proto_hbm, proto_ref, load_sem.at[0])
    load_emb = pltpu.make_async_copy(emb_hbm, emb_ref, load_sem.at[1])
    load_proto.start()
    load_emb.start()

    barrier = pltpu.get_barrier_semaphore()

    def greet(device):
        pl.semaphore_signal(barrier, inc=1, device_id=device, device_id_type=MESH)

    for d in far_first(nx):
        greet(at_x(lax.rem(x + d, nx)))
    for d in far_first(ny):
        for core in range(2):
            greet((x, lax.rem(y + d, ny) * (2 * ny) + z * 2 + core))
        greet((x, y * (2 * ny) + lax.rem(z + d, ny) * 2 + c))
    greet(sibling)
    greetings = nx - 1 + 3 * (ny - 1) + 1

    pending = []

    def sent(stage, ref):
        pending.append(pltpu.make_async_copy(ref, ref, send_sem.at[stage]))

    def flush():
        for copy in pending:
            copy.wait()
        pending.clear()

    def send(stage, source, place, device, received=None):
        pltpu.make_async_remote_copy(
            src_ref=source,
            dst_ref=place,
            send_sem=send_sem.at[stage],
            recv_sem=recv_sem.at[stage] if received is None else received,
            device_id=device,
            device_id_type=MESH,
        ).start()

    def broadcast(stage, count, me, at, buf):
        for d in far_first(count):
            send(stage, buf.at[me], buf.at[me], at(lax.rem(me + d, count)))
        sent(stage, buf.at[pl.ds(0, count - 1)])

    def arrived(stage, ref):
        pltpu.make_async_copy(ref, ref, recv_sem.at[stage]).wait()

    def gathered(stage, count, buf):
        arrived(stage, buf.at[pl.ds(0, count - 1)])

    def total_of(ref, count):
        total = ref[0]
        for j in range(1, count):
            total = total + ref[j]
        return total

    def fold(block):
        return jnp.sum(block.reshape(-1, SUB, LANES), axis=0)

    def across_lanes(block):
        return jnp.sum(fold(block.T), axis=0, keepdims=True)

    def store_columns(ref, tile):
        for r in range(SUB):
            ref[r * LANES : (r + 1) * LANES, :] = jnp.broadcast_to(tile[r : r + 1, :], (LANES, LANES)).T

    lane = [slice(j * LANES, (j + 1) * LANES) for j in range(tiles)]
    step = min(256, half)

    load_proto.wait()
    unit_proto, _ = normalize_rows(proto_ref[...])
    pb_ref[...] = unit_proto.astype(BF16)
    load_emb.wait()
    col = col_buf.at[0]
    for v in range(2):
        sums = [None] * tiles
        for i in range(v * half, (v + 1) * half, step):
            unit, _ = normalize_rows(emb_ref[i : i + step, :])
            eb = unit.astype(BF16)
            eb_ref[i : i + step, :] = eb
            s = lax.dot_general(eb, pb_ref[...], (((1,), (1,)), ((), ())), preferred_element_type=F32)
            soft = jnp.exp(s * INV_TEMPER)
            soft_ref[i : i + step, :] = soft
            for j in range(tiles):
                part = fold(soft[:, lane[j]] * soft[:, lane[j]])
                sums[j] = part if sums[j] is None else sums[j] + part
        for j in range(tiles):
            k = v * tiles + j
            col[x, k : k + 1, :] = jnp.sum(sums[j], axis=0, keepdims=True)

    pl.semaphore_wait(barrier, greetings)

    def row_sums(buf, scale):
        for r in range(SUB):
            v = r // tiles
            block = slice(r * LANES, (r + 1) * LANES)
            total = None
            for j in range(tiles):
                k = v * tiles + j
                part = sink_ref[block, lane[j]] * scale[k : k + 1, :]
                total = part if total is None else total + part
            buf[pos, r : r + 1, :] = across_lanes(total)

    soft_total = None
    weights = None
    scale = None
    extra = row_buf.at[ITERS]
    extraz = rowz_buf.at[ITERS]
    for sweep in range(ITERS):
        col = col_buf.at[sweep]
        if sweep > 0:
            for v in range(2):
                sums = [None] * tiles
                for i in range(v * half, (v + 1) * half, 64):
                    weight = wcol_ref[i : i + 64, :]
                    for j in range(tiles):
                        part = fold(sink_ref[i : i + 64, lane[j]] * weight)
                        sums[j] = part if sums[j] is None else sums[j] + part
                for j in range(tiles):
                    k = v * tiles + j
                    col[x, k : k + 1, :] = jnp.sum(sums[j], axis=0, keepdims=True)
        stage = 3 * sweep
        broadcast(stage, nx, x, at_x, col)
        if sweep == 0:
            for r in range(SUB):
                block = slice(r * LANES, (r + 1) * LANES)
                total = None
                for j in range(tiles):
                    soft = soft_ref[block, lane[j]]
                    sink_ref[block, lane[j]] = soft * soft
                    total = soft if total is None else total + soft
                extra[pos, r : r + 1, :] = across_lanes(total)
            broadcast(9, 2 * ny, pos, at_yc, extra)
        gathered(stage, nx, col)
        scale = 1.0 / total_of(col, nx)
        row = row_buf.at[sweep]
        row_sums(row, scale)
        broadcast(stage + 1, 2 * ny, pos, at_yc, row)
        if sweep == 0:
            gathered(9, 2 * ny, extra)
            extraz[z] = total_of(extra, 2 * ny)
            broadcast(10, ny, z, at_z, extraz)
        gathered(stage + 1, 2 * ny, row)
        rowz = rowz_buf.at[sweep]
        rowz[z] = total_of(row, 2 * ny)
        broadcast(stage + 2, ny, z, at_z, rowz)
        if sweep == 1:
            gathered(10, ny, extraz)
            soft_total = total_of(extraz, ny)
            store_columns(tcol_ref, INV_TEMPER / soft_total)
        if sweep == ITERS - 1:
            scale_ref[...] = scale * INV_TEMPER
        flush()
        gathered(stage + 2, ny, rowz)
        weights = 1.0 / total_of(rowz, ny)
        store_columns(wcol_ref, weights)

    def slopes(v, start):
        mine = pl.multiple_of(v * half + start, step)
        other = pl.multiple_of((1 - v) * half + start, step)
        for i in range(0, step, LANES):
            here = pl.ds(mine + i, LANES)
            there = pl.ds(other + i, LANES)
            weight = wcol_ref[there, :]
            share = tcol_ref[here, :]
            for j in range(tiles):
                pull = sink_ref[there, lane[j]] * scale_ref[pl.ds((1 - v) * tiles + j, 1), :] * weight
                slope_ref[here, lane[j]] = (soft_ref[here, lane[j]] * share - pull).astype(BF16)
        here = pl.ds(mine, step)
        epart_ref[here, :] = jnp.dot(slope_ref[here, :], pb_ref[...], preferred_element_type=F32)

    pieces = half // step
    per_piece = ny // pieces

    def piece(i, index):
        return lax.rem(index // per_piece + 1 + i, pieces)

    for i in range(pieces):
        start = piece(i, bi) * step
        slopes(1 - c, start)
        send(
            11,
            epart_ref.at[pl.ds((1 - c) * half + start, step)],
            sib_buf.at[pl.ds(start, step)],
            sibling,
            ring_sem.at[16 + i],
        )
    sent(11, sib_buf)
    for i in range(pieces):
        slopes(c, piece(i, ai) * step)

    for i in range(pieces):
        which = piece(i, ai)
        part = sib_buf.at[pl.ds(which * step, step)]
        pltpu.make_async_copy(part, part, ring_sem.at[16 + i]).wait()
        part[...] = part[...] + epart_ref[pl.ds(c * half + which * step, step), :]
        for d in range(1 if i == pieces - 1 else 0, per_piece):
            j = which * per_piece + lax.rem(ai + d, per_piece)
            send(13, sib_buf.at[pl.ds(j * ablock, ablock)], a_buf.at[ai], at_a(j))
    sent(13, a_buf.at[pl.ds(0, ny - 1)])
    a_buf[ai] = sib_buf[pl.ds(ai * ablock, ablock), :]

    for k in range(0, cols, LANES):
        ppart_ref[k : k + LANES, :] = lax.dot_general(
            slope_ref[:, k : k + LANES], eb_ref[...], (((0,), (0,)), ((), ())), preferred_element_type=F32
        )
    for d in far_first(nx):
        j = lax.rem(x + d, nx)
        send(12, ppart_ref.at[pl.ds(j * xblock, xblock)], x_buf.at[x], at_x(j))
    sent(12, x_buf.at[pl.ds(0, nx - 1)])
    x_buf[x] = ppart_ref[pl.ds(x * xblock, xblock), :]

    cross = row_buf.at[ITERS + 1]
    for v in range(2):
        for i in range(0, half, step):
            here = slice(v * half + i, v * half + i + step)
            s = lax.dot_general(
                eb_ref[here, :], pb_ref[...], (((1,), (1,)), ((), ())), preferred_element_type=F32
            )
            for q in range(0, step, LANES):
                other = slice((1 - v) * half + i + q, (1 - v) * half + i + q + LANES)
                total = None
                for j in range(tiles):
                    k = (1 - v) * tiles + j
                    part = sink_ref[other, lane[j]] * scale_ref[k : k + 1, :] * s[q : q + LANES, lane[j]]
                    total = part if total is None else total + part
                r = (v * half + i + q) // LANES
                cross[pos, r : r + 1, :] = across_lanes(total)
    broadcast(14, 2 * ny, pos, at_yc, cross)

    gathered(13, ny, a_buf)
    b_buf[bi] = total_of(a_buf, ny)
    broadcast(15, ny, bi, at_b, b_buf)

    crossz = rowz_buf.at[ITERS + 1]
    gathered(14, 2 * ny, cross)
    crossz[z] = total_of(cross, 2 * ny)
    broadcast(16, ny, z, at_z, crossz)

    own = pl.ds(x * xblock, xblock)
    unit, inverse = normalize_rows(proto_ref[own, :])
    gathered(12, nx, x_buf)
    gp_ref[own, :] = project(total_of(x_buf, nx), unit, inverse).astype(BF16)
    for d in far_first(nx):
        send(17, gp_ref.at[own], gp_ref.at[own], at_x(lax.rem(x + d, nx)))
    sent(17, gp_ref.at[pl.ds(0, (nx - 1) * xblock)])

    own = pl.ds(c * half + ai * ablock, ablock)
    unit, inverse = normalize_rows(emb_ref[own, :])
    gathered(15, ny, b_buf)
    ge_ref[own, :] = project(total_of(b_buf, ny), unit, inverse).astype(BF16)
    for d in far_first(ny):
        send(18, ge_ref.at[own], ge_ref.at[own], at_a(lax.rem(ai + d, ny)), ring_sem.at[ai])
    sent(18, ge_ref.at[pl.ds(0, (ny - 1) * ablock)])
    send(19, ge_ref.at[own], ge_ref.at[own], sibling)

    gathered(16, ny, crossz)
    swapped = jnp.concatenate([weights[tiles:], weights[:tiles]], axis=0)
    loss = jnp.log(soft_total) - total_of(crossz, ny) * swapped
    for v in range(2):
        for j in range(tiles):
            loss_ref[v : v + 1, lane[j]] = loss[v * tiles + j : v * tiles + j + 1, :]

    for d in reversed(far_first(ny)):
        j = lax.rem(ai + d, ny)
        block = ge_ref.at[pl.ds(c * half + j * ablock, ablock)]
        pltpu.make_async_copy(block, block, ring_sem.at[j]).wait()
        send(19, block, block, sibling)
    sent(19, ge_ref.at[pl.ds(0, half)])
    arrived(17, gp_ref.at[pl.ds(0, (nx - 1) * xblock)])
    flush()
    arrived(19, ge_ref.at[pl.ds(0, half)])


def finish(ge_ref, gp_ref, loss_ref, ge_out, gp_out, loss_out, sem):
    copies = [
        pltpu.make_async_copy(ge_ref, ge_out, sem.at[0]),
        pltpu.make_async_copy(gp_ref, gp_out, sem.at[1]),
        pltpu.make_async_copy(loss_ref, loss_out, sem.at[2]),
    ]
    for copy in copies:
        copy.start()
    for copy in copies:
        copy.wait()


def body(nx, ny, embeddings, prototypes):
    views, samples, width = embeddings.shape
    rows, cols = views * samples, prototypes.shape[0]
    ablock, xblock = samples // ny, cols // nx
    vmem = pl.BlockSpec(memory_space=pltpu.VMEM)
    hbm = pl.BlockSpec(memory_space=pltpu.HBM)
    shapes = (
        jax.ShapeDtypeStruct((rows, width), BF16),
        jax.ShapeDtypeStruct((cols, width), BF16),
        jax.ShapeDtypeStruct((views, samples), F32),
    )
    results = pl.pallas_call(
        functools.partial(kernel, nx, ny),
        out_shape=shapes,
        in_specs=[hbm, hbm],
        out_specs=(vmem, vmem, vmem),
        scratch_shapes=[
            pltpu.VMEM((rows, width), BF16),
            pltpu.VMEM((cols, width), BF16),
            pltpu.VMEM((rows, width), BF16),
            pltpu.VMEM((cols, width), BF16),
            pltpu.VMEM((rows, cols), F32),
            pltpu.VMEM((rows, cols), F32),
            pltpu.VMEM((rows, cols), BF16),
            pltpu.VMEM((rows, width), F32),
            pltpu.VMEM((cols, width), F32),
            pltpu.VMEM((rows, LANES), F32),
            pltpu.VMEM((rows, LANES), F32),
            pltpu.VMEM((SUB, LANES), F32),
            pltpu.VMEM((ITERS, nx, SUB, LANES), F32),
            pltpu.VMEM((ITERS + 2, 2 * ny, SUB, LANES), F32),
            pltpu.VMEM((ITERS + 2, ny, SUB, LANES), F32),
            pltpu.VMEM((samples, width), F32),
            pltpu.VMEM((ny, ablock, width), F32),
            pltpu.VMEM((ny, ablock, width), F32),
            pltpu.VMEM((nx, xblock, width), F32),
            pltpu.SemaphoreType.DMA((2,)),
            pltpu.SemaphoreType.DMA((20,)),
            pltpu.SemaphoreType.DMA((20,)),
            pltpu.SemaphoreType.DMA((24,)),
        ],
        compiler_params=pltpu.CompilerParams(
            collective_id=0, has_side_effects=True, vmem_limit_bytes=48 * 2**20
        ),
    )(embeddings.reshape(rows, width), prototypes)
    ge, gp, loss = pl.pallas_call(
        finish,
        out_shape=shapes,
        in_specs=[vmem, vmem, vmem],
        out_specs=(hbm, hbm, hbm),
        scratch_shapes=[pltpu.SemaphoreType.DMA((3,))],
        compiler_params=pltpu.CompilerParams(vmem_limit_bytes=8 * 2**20),
    )(*results)
    return ge.reshape(views, samples, width), gp, loss


def solution(mesh):
    nx = mesh.shape["samp"]
    ny = 1
    while 2 * ny * ny < mesh.shape["proto"]:
        ny += 1
    return jax.shard_map(
        functools.partial(body, nx, ny),
        mesh=mesh,
        in_specs=(P(None, "samp", None), P("proto", None)),
        out_specs=(P(None, "samp", None), P("proto", None), P(None, "samp")),
        check_vma=False,
    )
```

```python
import functools

import jax
import jax.numpy as jnp
from jax import lax
from jax.experimental import pallas as pl
from jax.experimental.pallas import tpu as pltpu
from jax.sharding import PartitionSpec as P

ITERS = 3
INV_TEMPER = 10.0
F32 = jnp.float32
BF16 = jnp.bfloat16
MESH = pl.DeviceIdType.MESH
LANES = 128
SUB = 8
SOFT = 9
SIBLING_SUM = 11
PROTO_RS = 13
PROTO_AG = 15
EMB_A = 17
EMB_B = 19
EMB_AG = 21
TO_SIBLING = 23
CROSS = 25
STAGES = 27


def normalize_rows(values):
    as_float = values.astype(F32)
    inverse = lax.rsqrt(jnp.sum(as_float * as_float, axis=-1, keepdims=True) + 1e-06)
    return as_float * inverse, inverse


def project(summed, unit_rows, inverse):
    return (summed - unit_rows * jnp.sum(unit_rows * summed, axis=-1, keepdims=True)) * inverse


def far_first(count):
    half = count // 2
    order = [half]
    for step in range(1, half + 1):
        for offset in (half - step, half + step):
            if 0 < offset < count and offset not in order:
                order.append(offset)
    return order


def kernel(
    nx,
    ny,
    emb_hbm,
    proto_hbm,
    ge_ref,
    gp_ref,
    loss_ref,
    emb_ref,
    proto_ref,
    eb_ref,
    pb_ref,
    soft_ref,
    sink_ref,
    slope_ref,
    epart_ref,
    ppart_ref,
    wcol_ref,
    tcol_ref,
    scale_ref,
    col_buf,
    row_buf,
    rowz_buf,
    sib_buf,
    a_buf,
    b_buf,
    x_buf,
    load_sem,
    send_sem,
    recv_sem,
    ring_sem,
):
    rows, width = eb_ref.shape
    half = rows // 2
    cols = pb_ref.shape[0]
    tiles = cols // LANES
    x = lax.axis_index("samp")
    p = lax.axis_index("proto")
    y = p // (2 * ny)
    z = (p // 2) % ny
    c = p % 2
    pos = y * 2 + c
    ai = y + (z - y) * c
    bi = z + (y - z) * c
    astep = 2 * ny + (2 - 2 * ny) * c
    bstep = 2 + (2 * ny - 2) * c
    step = half // 2
    xstep = cols // 2
    aq = step // ny
    xq = xstep // nx

    def at_x(j):
        return (j, p)

    def at_yc(j):
        return (x, (j // 2) * (2 * ny) + z * 2 + j % 2)

    def at_z(j):
        return (x, y * (2 * ny) + j * 2 + c)

    def at_a(j):
        return (x, p + (j - ai) * astep)

    def at_b(j):
        return (x, p + (j - bi) * bstep)

    sibling = (x, p + 1 - 2 * c)

    load_proto = pltpu.make_async_copy(proto_hbm, proto_ref, load_sem.at[0])
    load_emb = pltpu.make_async_copy(emb_hbm, emb_ref, load_sem.at[1])
    load_proto.start()
    load_emb.start()

    barrier = pltpu.get_barrier_semaphore()

    def greet(device):
        pl.semaphore_signal(barrier, inc=1, device_id=device, device_id_type=MESH)

    for d in far_first(nx):
        greet(at_x(lax.rem(x + d, nx)))
    for d in far_first(ny):
        for core in range(2):
            greet((x, lax.rem(y + d, ny) * (2 * ny) + z * 2 + core))
        greet((x, y * (2 * ny) + lax.rem(z + d, ny) * 2 + c))
    greet(sibling)
    greetings = nx - 1 + 3 * (ny - 1) + 1

    pending = []

    def sent(stage, ref):
        pending.append(pltpu.make_async_copy(ref, ref, send_sem.at[stage]))

    def flush():
        for copy in pending:
            copy.wait()
        pending.clear()

    def send(stage, source, place, device, received=None):
        pltpu.make_async_remote_copy(
            src_ref=source,
            dst_ref=place,
            send_sem=send_sem.at[stage],
            recv_sem=recv_sem.at[stage] if received is None else received,
            device_id=device,
            device_id_type=MESH,
        ).start()

    def broadcast(stage, count, me, at, buf):
        for d in far_first(count):
            send(stage, buf.at[me], buf.at[me], at(lax.rem(me + d, count)))
        sent(stage, buf.at[pl.ds(0, count - 1)])

    def arrived(stage, ref):
        pltpu.make_async_copy(ref, ref, recv_sem.at[stage]).wait()

    def gathered(stage, count, buf):
        arrived(stage, buf.at[pl.ds(0, count - 1)])

    def total_of(ref, count):
        total = ref[0]
        for j in range(1, count):
            total = total + ref[j]
        return total

    def fold(block):
        return jnp.sum(block.reshape(-1, SUB, LANES), axis=0)

    def across_lanes(block):
        return jnp.sum(fold(block.T), axis=0, keepdims=True)

    def store_columns(ref, tile):
        for r in range(SUB):
            ref[r * LANES : (r + 1) * LANES, :] = jnp.broadcast_to(tile[r : r + 1, :], (LANES, LANES)).T

    lane = [slice(j * LANES, (j + 1) * LANES) for j in range(tiles)]

    load_proto.wait()
    unit_proto, _ = normalize_rows(proto_ref[...])
    pb_ref[...] = unit_proto.astype(BF16)
    load_emb.wait()
    col = col_buf.at[0]
    for v in range(2):
        sums = [None] * tiles
        for i in range(v * half, (v + 1) * half, step):
            unit, _ = normalize_rows(emb_ref[i : i + step, :])
            eb = unit.astype(BF16)
            eb_ref[i : i + step, :] = eb
            s = lax.dot_general(eb, pb_ref[...], (((1,), (1,)), ((), ())), preferred_element_type=F32)
            soft = jnp.exp(s * INV_TEMPER)
            soft_ref[i : i + step, :] = soft
            for j in range(tiles):
                part = fold(soft[:, lane[j]] * soft[:, lane[j]])
                sums[j] = part if sums[j] is None else sums[j] + part
        for j in range(tiles):
            k = v * tiles + j
            col[x, k : k + 1, :] = jnp.sum(sums[j], axis=0, keepdims=True)

    pl.semaphore_wait(barrier, greetings)

    def row_sums(buf, scale):
        for r in range(SUB):
            v = r // tiles
            block = slice(r * LANES, (r + 1) * LANES)
            total = None
            for j in range(tiles):
                k = v * tiles + j
                part = sink_ref[block, lane[j]] * scale[k : k + 1, :]
                total = part if total is None else total + part
            buf[pos, r : r + 1, :] = across_lanes(total)

    soft_total = None
    weights = None
    scale = None
    extra = row_buf.at[ITERS]
    extraz = rowz_buf.at[ITERS]
    for sweep in range(ITERS):
        col = col_buf.at[sweep]
        if sweep > 0:
            for v in range(2):
                sums = [None] * tiles
                for i in range(v * half, (v + 1) * half, 64):
                    weight = wcol_ref[i : i + 64, :]
                    for j in range(tiles):
                        part = fold(sink_ref[i : i + 64, lane[j]] * weight)
                        sums[j] = part if sums[j] is None else sums[j] + part
                for j in range(tiles):
                    k = v * tiles + j
                    col[x, k : k + 1, :] = jnp.sum(sums[j], axis=0, keepdims=True)
        stage = 3 * sweep
        broadcast(stage, nx, x, at_x, col)
        if sweep == 0:
            for r in range(SUB):
                block = slice(r * LANES, (r + 1) * LANES)
                total = None
                for j in range(tiles):
                    soft = soft_ref[block, lane[j]]
                    sink_ref[block, lane[j]] = soft * soft
                    total = soft if total is None else total + soft
                extra[pos, r : r + 1, :] = across_lanes(total)
            broadcast(SOFT, 2 * ny, pos, at_yc, extra)
        gathered(stage, nx, col)
        scale = 1.0 / total_of(col, nx)
        row = row_buf.at[sweep]
        row_sums(row, scale)
        broadcast(stage + 1, 2 * ny, pos, at_yc, row)
        if sweep == 0:
            gathered(SOFT, 2 * ny, extra)
            extraz[z] = total_of(extra, 2 * ny)
            broadcast(SOFT + 1, ny, z, at_z, extraz)
        gathered(stage + 1, 2 * ny, row)
        rowz = rowz_buf.at[sweep]
        rowz[z] = total_of(row, 2 * ny)
        broadcast(stage + 2, ny, z, at_z, rowz)
        if sweep == 1:
            gathered(SOFT + 1, ny, extraz)
            soft_total = total_of(extraz, ny)
            store_columns(tcol_ref, INV_TEMPER / soft_total)
        if sweep == ITERS - 1:
            scale_ref[...] = scale * INV_TEMPER
        flush()
        gathered(stage + 2, ny, rowz)
        weights = 1.0 / total_of(rowz, ny)
        store_columns(wcol_ref, weights)

    def slopes(v, h):
        mine = pl.multiple_of(v * half + h * step, step)
        other = pl.multiple_of((1 - v) * half + h * step, step)
        for i in range(0, step, LANES):
            here = pl.ds(mine + i, LANES)
            there = pl.ds(other + i, LANES)
            weight = wcol_ref[there, :]
            share = tcol_ref[here, :]
            for j in range(tiles):
                pull = sink_ref[there, lane[j]] * scale_ref[pl.ds((1 - v) * tiles + j, 1), :] * weight
                slope_ref[here, lane[j]] = (soft_ref[here, lane[j]] * share - pull).astype(BF16)
        here = pl.ds(mine, step)
        epart_ref[here, :] = jnp.dot(slope_ref[here, :], pb_ref[...], preferred_element_type=F32)

    def proto_terms(h):
        for k in range(h * xstep, (h + 1) * xstep, LANES):
            ppart_ref[k : k + LANES, :] = lax.dot_general(
                slope_ref[:, k : k + LANES], eb_ref[...], (((0,), (0,)), ((), ())), preferred_element_type=F32
            )
        for d in far_first(nx):
            j = lax.rem(x + d, nx)
            send(PROTO_RS + h, ppart_ref.at[pl.ds(h * xstep + j * xq, xq)], x_buf.at[h, x], at_x(j))
        sent(PROTO_RS + h, x_buf.at[h, pl.ds(0, nx - 1)])
        x_buf[h, x] = ppart_ref[pl.ds(h * xstep + x * xq, xq), :]

    def proto_result(h):
        own = pl.ds(h * xstep + x * xq, xq)
        unit, inverse = normalize_rows(proto_ref[own, :])
        gathered(PROTO_RS + h, nx, x_buf.at[h])
        gp_ref[own, :] = project(total_of(x_buf.at[h], nx), unit, inverse).astype(BF16)
        for d in far_first(nx):
            send(PROTO_AG + h, gp_ref.at[own], gp_ref.at[own], at_x(lax.rem(x + d, nx)))
        sent(PROTO_AG + h, gp_ref.at[pl.ds(0, (nx - 1) * xq)])

    def emb_result(h):
        own = pl.ds(c * half + h * step + ai * aq, aq)
        unit, inverse = normalize_rows(emb_ref[own, :])
        gathered(EMB_B + h, ny, b_buf.at[h])
        ge_ref[own, :] = project(total_of(b_buf.at[h], ny), unit, inverse).astype(BF16)
        block = ge_ref.at[own]
        for d in far_first(ny):
            send(EMB_AG + h, block, block, at_a(lax.rem(ai + d, ny)), ring_sem.at[h, ai])
        sent(EMB_AG + h, ge_ref.at[pl.ds(0, (ny - 1) * aq)])
        send(TO_SIBLING + h, block, block, sibling)

    for h in range(2):
        slopes(1 - c, h)
        part = pl.ds(h * step, step)
        send(SIBLING_SUM + h, epart_ref.at[pl.ds((1 - c) * half + h * step, step)], sib_buf.at[part], sibling)
        sent(SIBLING_SUM + h, sib_buf.at[part])
    for h in range(2):
        slopes(c, h)
    proto_terms(0)
    for h in range(2):
        part = pl.ds(h * step, step)
        arrived(SIBLING_SUM + h, sib_buf.at[part])
        sib_buf[part, :] = sib_buf[part, :] + epart_ref[pl.ds(c * half + h * step, step), :]
        for d in far_first(ny):
            j = lax.rem(ai + d, ny)
            send(EMB_A + h, sib_buf.at[pl.ds(h * step + j * aq, aq)], a_buf.at[h, ai], at_a(j))
        sent(EMB_A + h, a_buf.at[h, pl.ds(0, ny - 1)])
        a_buf[h, ai] = sib_buf[pl.ds(h * step + ai * aq, aq), :]
    proto_terms(1)

    cross = row_buf.at[ITERS + 1]
    for v in range(2):
        for i in range(0, half, step):
            here = slice(v * half + i, v * half + i + step)
            s = lax.dot_general(
                eb_ref[here, :], pb_ref[...], (((1,), (1,)), ((), ())), preferred_element_type=F32
            )
            for q in range(0, step, LANES):
                other = slice((1 - v) * half + i + q, (1 - v) * half + i + q + LANES)
                total = None
                for j in range(tiles):
                    k = (1 - v) * tiles + j
                    part = sink_ref[other, lane[j]] * scale_ref[k : k + 1, :] * s[q : q + LANES, lane[j]]
                    total = part if total is None else total + part
                r = (v * half + i + q) // LANES
                cross[pos, r : r + 1, :] = across_lanes(total)
    broadcast(CROSS, 2 * ny, pos, at_yc, cross)

    for h in range(2):
        gathered(EMB_A + h, ny, a_buf.at[h])
        b_buf[h, bi] = total_of(a_buf.at[h], ny)
        broadcast(EMB_B + h, ny, bi, at_b, b_buf.at[h])

    proto_result(0)
    crossz = rowz_buf.at[ITERS + 1]
    gathered(CROSS, 2 * ny, cross)
    crossz[z] = total_of(cross, 2 * ny)
    broadcast(CROSS + 1, ny, z, at_z, crossz)
    emb_result(0)
    proto_result(1)
    emb_result(1)

    gathered(CROSS + 1, ny, crossz)
    swapped = jnp.concatenate([weights[tiles:], weights[:tiles]], axis=0)
    loss = jnp.log(soft_total) - total_of(crossz, ny) * swapped
    for v in range(2):
        for j in range(tiles):
            loss_ref[v : v + 1, lane[j]] = loss[v * tiles + j : v * tiles + j + 1, :]

    for h in range(2):
        for d in reversed(far_first(ny)):
            j = lax.rem(ai + d, ny)
            block = ge_ref.at[pl.ds(c * half + h * step + j * aq, aq)]
            pltpu.make_async_copy(block, block, ring_sem.at[h, j]).wait()
            send(TO_SIBLING + h, block, block, sibling)
        sent(TO_SIBLING + h, ge_ref.at[pl.ds(0, step)])
    for h in range(2):
        arrived(PROTO_AG + h, gp_ref.at[pl.ds(0, (nx - 1) * xq)])
    flush()
    for h in range(2):
        arrived(TO_SIBLING + h, ge_ref.at[pl.ds(0, step)])


def finish(ge_ref, gp_ref, loss_ref, ge_out, gp_out, loss_out, sem):
    copies = [
        pltpu.make_async_copy(ge_ref, ge_out, sem.at[0]),
        pltpu.make_async_copy(gp_ref, gp_out, sem.at[1]),
        pltpu.make_async_copy(loss_ref, loss_out, sem.at[2]),
    ]
    for copy in copies:
        copy.start()
    for copy in copies:
        copy.wait()


def body(nx, ny, embeddings, prototypes):
    views, samples, width = embeddings.shape
    rows, cols = views * samples, prototypes.shape[0]
    aq, xq = samples // 2 // ny, cols // 2 // nx
    vmem = pl.BlockSpec(memory_space=pltpu.VMEM)
    hbm = pl.BlockSpec(memory_space=pltpu.HBM)
    shapes = (
        jax.ShapeDtypeStruct((rows, width), BF16),
        jax.ShapeDtypeStruct((cols, width), BF16),
        jax.ShapeDtypeStruct((views, samples), F32),
    )
    results = pl.pallas_call(
        functools.partial(kernel, nx, ny),
        out_shape=shapes,
        in_specs=[hbm, hbm],
        out_specs=(vmem, vmem, vmem),
        scratch_shapes=[
            pltpu.VMEM((rows, width), BF16),
            pltpu.VMEM((cols, width), BF16),
            pltpu.VMEM((rows, width), BF16),
            pltpu.VMEM((cols, width), BF16),
            pltpu.VMEM((rows, cols), F32),
            pltpu.VMEM((rows, cols), F32),
            pltpu.VMEM((rows, cols), BF16),
            pltpu.VMEM((rows, width), F32),
            pltpu.VMEM((cols, width), F32),
            pltpu.VMEM((rows, LANES), F32),
            pltpu.VMEM((rows, LANES), F32),
            pltpu.VMEM((SUB, LANES), F32),
            pltpu.VMEM((ITERS, nx, SUB, LANES), F32),
            pltpu.VMEM((ITERS + 2, 2 * ny, SUB, LANES), F32),
            pltpu.VMEM((ITERS + 2, ny, SUB, LANES), F32),
            pltpu.VMEM((samples, width), F32),
            pltpu.VMEM((2, ny, aq, width), F32),
            pltpu.VMEM((2, ny, aq, width), F32),
            pltpu.VMEM((2, nx, xq, width), F32),
            pltpu.SemaphoreType.DMA((2,)),
            pltpu.SemaphoreType.DMA((STAGES,)),
            pltpu.SemaphoreType.DMA((STAGES,)),
            pltpu.SemaphoreType.DMA((2, ny)),
        ],
        compiler_params=pltpu.CompilerParams(
            collective_id=0, has_side_effects=True, vmem_limit_bytes=48 * 2**20
        ),
    )(
        pltpu.with_memory_space_constraint(embeddings.reshape(rows, width), pltpu.HBM),
        pltpu.with_memory_space_constraint(prototypes, pltpu.HBM),
    )
    ge, gp, loss = pl.pallas_call(
        finish,
        out_shape=shapes,
        in_specs=[vmem, vmem, vmem],
        out_specs=(hbm, hbm, hbm),
        scratch_shapes=[pltpu.SemaphoreType.DMA((3,))],
        compiler_params=pltpu.CompilerParams(vmem_limit_bytes=8 * 2**20),
    )(*results)
    return ge.reshape(views, samples, width), gp, loss


def solution(mesh):
    nx = mesh.shape["samp"]
    ny = 1
    while 2 * ny * ny < mesh.shape["proto"]:
        ny += 1
    return jax.shard_map(
        functools.partial(body, nx, ny),
        mesh=mesh,
        in_specs=(P(None, "samp", None), P("proto", None)),
        out_specs=(P(None, "samp", None), P("proto", None), P(None, "samp")),
        check_vma=False,
    )
```

```python
import functools

import jax
import jax.numpy as jnp
from jax import lax
from jax.experimental import pallas as pl
from jax.experimental.pallas import tpu as pltpu
from jax.sharding import PartitionSpec as P

ITERS = 3
INV_TEMPER = 10.0
F32 = jnp.float32
BF16 = jnp.bfloat16
MESH = pl.DeviceIdType.MESH
LANES = 128
SUB = 8
SOFT = 9
PROTO_RS = 11
PROTO_AG = 13
EMB_B = 15
EMB_AG = 17
TO_SIBLING = 19
CROSS = 21
SCALES = 23
PAIR = 24
RING = 25
STAGES = 29


def normalize_rows(values):
    as_float = values.astype(F32)
    inverse = lax.rsqrt(jnp.sum(as_float * as_float, axis=-1, keepdims=True) + 1e-06)
    return as_float * inverse, inverse


def project(summed, unit_rows, inverse):
    return (summed - unit_rows * jnp.sum(unit_rows * summed, axis=-1, keepdims=True)) * inverse


def far_first(count):
    half = count // 2
    order = [half]
    for step in range(1, half + 1):
        for offset in (half - step, half + step):
            if 0 < offset < count and offset not in order:
                order.append(offset)
    return order


def kernel(
    nx,
    ny,
    emb_hbm,
    proto_hbm,
    ge_ref,
    gp_ref,
    loss_ref,
    emb_ref,
    proto_ref,
    eb_ref,
    pb_ref,
    soft_ref,
    sink_ref,
    slope_ref,
    ring_ref,
    ring_soft,
    ring_sink,
    ring_slope,
    ppart_ref,
    wcol_ref,
    tcol_ref,
    scale_ref,
    col_buf,
    row_buf,
    rowz_buf,
    scales_buf,
    b_buf,
    x_buf,
    load_sem,
    send_sem,
    recv_sem,
    ring_sem,
    block_sem,
):
    rows, width = eb_ref.shape
    half = rows // 2
    cols = pb_ref.shape[0]
    tiles = cols // LANES
    x = lax.axis_index("samp")
    p = lax.axis_index("proto")
    y = p // (2 * ny)
    z = (p // 2) % ny
    c = p % 2
    pos = y * 2 + c
    ai = y + (z - y) * c
    bi = z + (y - z) * c
    astep = 2 * ny + (2 - 2 * ny) * c
    bstep = 2 + (2 * ny - 2) * c
    step = half // 2
    xstep = cols // 2
    aq = step // ny
    xq = xstep // nx

    def at_x(j):
        return (j, p)

    def at_yc(j):
        return (x, (j // 2) * (2 * ny) + z * 2 + j % 2)

    def at_z(j):
        return (x, y * (2 * ny) + j * 2 + c)

    def at_a(j):
        return (x, p + (j - ai) * astep)

    def at_b(j):
        return (x, p + (j - bi) * bstep)

    sibling = (x, p + 1 - 2 * c)

    load_proto = pltpu.make_async_copy(proto_hbm, proto_ref, load_sem.at[0])
    load_emb = pltpu.make_async_copy(emb_hbm, emb_ref, load_sem.at[1])
    load_proto.start()
    load_emb.start()

    barrier = pltpu.get_barrier_semaphore()

    def greet(device):
        pl.semaphore_signal(barrier, inc=1, device_id=device, device_id_type=MESH)

    for d in far_first(nx):
        greet(at_x(lax.rem(x + d, nx)))
    for d in far_first(ny):
        for core in range(2):
            greet((x, lax.rem(y + d, ny) * (2 * ny) + z * 2 + core))
            greet((x, y * (2 * ny) + lax.rem(z + d, ny) * 2 + core))
    greet(sibling)
    greetings = nx - 1 + 4 * (ny - 1) + 1

    pending = []

    def sent(stage, ref):
        pending.append(pltpu.make_async_copy(ref, ref, send_sem.at[stage]))

    def flush():
        for copy in pending:
            copy.wait()
        pending.clear()

    def send(stage, source, place, device, received=None):
        pltpu.make_async_remote_copy(
            src_ref=source,
            dst_ref=place,
            send_sem=send_sem.at[stage],
            recv_sem=recv_sem.at[stage] if received is None else received,
            device_id=device,
            device_id_type=MESH,
        ).start()

    def broadcast(stage, count, me, at, buf):
        for d in far_first(count):
            send(stage, buf.at[me], buf.at[me], at(lax.rem(me + d, count)))
        sent(stage, buf.at[pl.ds(0, count - 1)])

    def arrived(stage, ref):
        pltpu.make_async_copy(ref, ref, recv_sem.at[stage]).wait()

    def gathered(stage, count, buf):
        arrived(stage, buf.at[pl.ds(0, count - 1)])

    def total_of(ref, count):
        total = ref[0]
        for j in range(1, count):
            total = total + ref[j]
        return total

    def fold(block):
        return jnp.sum(block.reshape(-1, SUB, LANES), axis=0)

    def across_lanes(block):
        return jnp.sum(fold(block.T), axis=0, keepdims=True)

    def store_columns(ref, tile):
        for r in range(SUB):
            ref[r * LANES : (r + 1) * LANES, :] = jnp.broadcast_to(tile[r : r + 1, :], (LANES, LANES)).T

    lane = [slice(j * LANES, (j + 1) * LANES) for j in range(tiles)]

    load_proto.wait()
    unit_proto, _ = normalize_rows(proto_ref[...])
    pb_ref[...] = unit_proto.astype(BF16)
    ring_ref[ai, pl.ds(pl.multiple_of(c * cols, cols), cols), :] = pb_ref[...]
    load_emb.wait()
    col = col_buf.at[0]
    for v in range(2):
        sums = [None] * tiles
        for i in range(v * half, (v + 1) * half, step):
            unit, _ = normalize_rows(emb_ref[i : i + step, :])
            eb = unit.astype(BF16)
            eb_ref[i : i + step, :] = eb
            s = lax.dot_general(eb, pb_ref[...], (((1,), (1,)), ((), ())), preferred_element_type=F32)
            soft = jnp.exp(s * INV_TEMPER)
            soft_ref[i : i + step, :] = soft
            for j in range(tiles):
                part = fold(soft[:, lane[j]] * soft[:, lane[j]])
                sums[j] = part if sums[j] is None else sums[j] + part
        for j in range(tiles):
            k = v * tiles + j
            col[x, k : k + 1, :] = jnp.sum(sums[j], axis=0, keepdims=True)

    pl.semaphore_wait(barrier, greetings)

    right = lax.rem(ai + 1, ny)
    left = lax.rem(ai + ny - 1, ny)

    def slot(offset):
        return lax.rem(ai + offset + ny, ny)

    def pass_on(hop):
        back, ahead = slot(-hop), slot(hop)
        if hop < ny // 2 - 1:
            send(RING + hop, ring_ref.at[back], ring_ref.at[back], at_a(right), ring_sem.at[back])
            send(RING + hop, ring_ref.at[ahead], ring_ref.at[ahead], at_a(left), ring_sem.at[ahead])
            sent(RING + hop, ring_ref.at[pl.ds(0, 2)])
        else:
            for to, origin, half_of in ((right, back, 0), (left, ahead, 1)):
                block = ring_ref.at[origin, pl.ds(half_of * cols, cols)]
                send(RING + hop, block, block, at_a(to), ring_sem.at[origin])
            sent(RING + hop, ring_ref.at[0])

    def passed(offset):
        block = ring_ref.at[slot(offset)]
        pltpu.make_async_copy(block, block, ring_sem.at[slot(offset)]).wait()

    def ring_terms(offset):
        mine = eb_ref[pl.ds(pl.multiple_of(c * half + ai * 2 * aq, 2 * aq), 2 * aq), :]
        other = eb_ref[pl.ds(pl.multiple_of((1 - c) * half + ai * 2 * aq, 2 * aq), 2 * aq), :]
        both = jnp.concatenate([mine, other], axis=0)
        for k in range(0, 2 * cols, cols):
            s = lax.dot_general(
                both,
                ring_ref[slot(offset), k : k + cols, :],
                (((1,), (1,)), ((), ())),
                preferred_element_type=F32,
            )
            soft = jnp.exp(s * INV_TEMPER)
            ring_soft[offset % ny, :, k : k + cols] = soft[: 2 * aq]
            ring_sink[offset % ny, :, k : k + cols] = soft[2 * aq :] * soft[2 * aq :]

    def row_sums(buf, scale):
        for r in range(SUB):
            v = r // tiles
            block = slice(r * LANES, (r + 1) * LANES)
            total = None
            for j in range(tiles):
                k = v * tiles + j
                part = sink_ref[block, lane[j]] * scale[k : k + 1, :]
                total = part if total is None else total + part
            buf[pos, r : r + 1, :] = across_lanes(total)

    soft_total = None
    weights = None
    scale = None
    extra = row_buf.at[ITERS]
    extraz = rowz_buf.at[ITERS]
    for sweep in range(ITERS):
        col = col_buf.at[sweep]
        if sweep > 0:
            for v in range(2):
                sums = [None] * tiles
                for i in range(v * half, (v + 1) * half, 64):
                    weight = wcol_ref[i : i + 64, :]
                    for j in range(tiles):
                        part = fold(sink_ref[i : i + 64, lane[j]] * weight)
                        sums[j] = part if sums[j] is None else sums[j] + part
                for j in range(tiles):
                    k = v * tiles + j
                    col[x, k : k + 1, :] = jnp.sum(sums[j], axis=0, keepdims=True)
        stage = 3 * sweep
        broadcast(stage, nx, x, at_x, col)
        if sweep == 0:
            pair = ring_ref.at[ai, pl.ds(c * cols, cols)]
            send(PAIR, pair, ring_ref.at[bi, pl.ds(c * cols, cols)], sibling)
            sent(PAIR, pb_ref)
        if sweep == 1:
            ring_terms(1)
            ring_terms(-1)
        if sweep == 2:
            passed(3)
            passed(-3)
            pass_on(3)
            ring_terms(3)
            ring_terms(-3)
        if sweep == 0:
            for r in range(SUB):
                block = slice(r * LANES, (r + 1) * LANES)
                total = None
                for j in range(tiles):
                    soft = soft_ref[block, lane[j]]
                    sink_ref[block, lane[j]] = soft * soft
                    total = soft if total is None else total + soft
                extra[pos, r : r + 1, :] = across_lanes(total)
            broadcast(SOFT, 2 * ny, pos, at_yc, extra)
            arrived(PAIR, pb_ref)
            pass_on(0)
        gathered(stage, nx, col)
        scale = 1.0 / total_of(col, nx)
        row = row_buf.at[sweep]
        row_sums(row, scale)
        broadcast(stage + 1, 2 * ny, pos, at_yc, row)
        if sweep == 0:
            gathered(SOFT, 2 * ny, extra)
            extraz[z] = total_of(extra, 2 * ny)
            broadcast(SOFT + 1, ny, z, at_z, extraz)
            ring_terms(0)
        if sweep == 1:
            passed(2)
            passed(-2)
            pass_on(2)
        if sweep == 2:
            tens = scale * INV_TEMPER
            scale_ref[...] = tens
            scales_buf[ai * 2 + c] = tens
            for d in far_first(ny):
                send(SCALES, scale_ref, scales_buf.at[y * 2 + c], (x, lax.rem(y + d, ny) * (2 * ny) + z * 2))
                send(SCALES, scale_ref, scales_buf.at[z * 2 + c], (x, y * (2 * ny) + lax.rem(z + d, ny) * 2 + 1))
            send(SCALES, scale_ref, scales_buf.at[bi * 2 + c], sibling)
            sent(SCALES, scales_buf.at[pl.ds(0, 2 * ny - 1)])
        gathered(stage + 1, 2 * ny, row)
        rowz = rowz_buf.at[sweep]
        rowz[z] = total_of(row, 2 * ny)
        broadcast(stage + 2, ny, z, at_z, rowz)
        if sweep == 1:
            gathered(SOFT + 1, ny, extraz)
            soft_total = total_of(extraz, ny)
            store_columns(tcol_ref, INV_TEMPER / soft_total)
            ring_terms(2)
            ring_terms(-2)
        if sweep == 0:
            passed(1)
            passed(-1)
            pass_on(1)
        if sweep == 2:
            passed(4)
            ring_terms(4)
            gathered(SCALES, 2 * ny, scales_buf)
            flush()
        gathered(stage + 2, ny, rowz)
        weights = 1.0 / total_of(rowz, ny)
        store_columns(wcol_ref, weights)

    def slopes(v, h):
        mine = pl.multiple_of(v * half + h * step, step)
        other = pl.multiple_of((1 - v) * half + h * step, step)
        for i in range(0, step, LANES):
            here = pl.ds(mine + i, LANES)
            there = pl.ds(other + i, LANES)
            weight = wcol_ref[there, :]
            share = tcol_ref[here, :]
            for j in range(tiles):
                pull = sink_ref[there, lane[j]] * scale_ref[pl.ds((1 - v) * tiles + j, 1), :] * weight
                slope_ref[here, lane[j]] = (soft_ref[here, lane[j]] * share - pull).astype(BF16)

    def proto_terms(h):
        for k in range(h * xstep, (h + 1) * xstep, LANES):
            ppart_ref[k : k + LANES, :] = lax.dot_general(
                slope_ref[:, k : k + LANES], eb_ref[...], (((0,), (0,)), ((), ())), preferred_element_type=F32
            )
        for d in far_first(nx):
            j = lax.rem(x + d, nx)
            send(PROTO_RS + h, ppart_ref.at[pl.ds(h * xstep + j * xq, xq)], x_buf.at[h, x], at_x(j))
        sent(PROTO_RS + h, x_buf.at[h, pl.ds(0, nx - 1)])
        x_buf[h, x] = ppart_ref[pl.ds(h * xstep + x * xq, xq), :]

    def proto_result(h):
        own = pl.ds(h * xstep + x * xq, xq)
        unit, inverse = normalize_rows(proto_ref[own, :])
        gathered(PROTO_RS + h, nx, x_buf.at[h])
        gp_ref[own, :] = project(total_of(x_buf.at[h], nx), unit, inverse).astype(BF16)
        for d in far_first(nx):
            send(PROTO_AG + h, gp_ref.at[own], gp_ref.at[own], at_x(lax.rem(x + d, nx)))
        sent(PROTO_AG + h, gp_ref.at[pl.ds(0, (nx - 1) * xq)])

    def emb_result(h):
        own = pl.ds(c * half + (2 * ai + h) * aq, aq)
        unit, inverse = normalize_rows(emb_ref[own, :])
        gathered(EMB_B + h, ny, b_buf.at[h])
        ge_ref[own, :] = project(total_of(b_buf.at[h], ny), unit, inverse).astype(BF16)
        block = ge_ref.at[own]
        for d in far_first(ny):
            send(EMB_AG + h, block, block, at_a(lax.rem(ai + d, ny)), block_sem.at[h, ai])
        sent(EMB_AG + h, ge_ref.at[pl.ds(0, (ny - 1) * aq)])
        send(TO_SIBLING + h, block, block, sibling)

    share = tcol_ref[pl.ds(pl.multiple_of(c * half + ai * 2 * aq, 2 * aq), 2 * aq), :]
    weight = wcol_ref[pl.ds(pl.multiple_of((1 - c) * half + ai * 2 * aq, 2 * aq), 2 * aq), :]
    total = None
    for offset in range(ny):
        for k in range(2 * tiles):
            at = slice(k * LANES, (k + 1) * LANES)
            factor = scales_buf[slot(offset) * 2 + k // tiles, pl.ds((1 - c) * tiles + k % tiles, 1), :]
            pull = ring_sink[offset, :, at] * factor * weight
            ring_slope[offset, :, at] = (ring_soft[offset, :, at] * share - pull).astype(BF16)
        part = jnp.dot(ring_slope[offset], ring_ref[slot(offset)], preferred_element_type=F32)
        total = part if total is None else total + part
    for h in range(2):
        b_buf[h, bi] = total[h * aq : (h + 1) * aq]
        broadcast(EMB_B + h, ny, bi, at_b, b_buf.at[h])

    for v in range(2):
        for h in range(2):
            slopes(v, h)
    proto_terms(0)
    proto_terms(1)

    cross = row_buf.at[ITERS + 1]
    for v in range(2):
        for i in range(0, half, step):
            here = slice(v * half + i, v * half + i + step)
            s = lax.dot_general(
                eb_ref[here, :], pb_ref[...], (((1,), (1,)), ((), ())), preferred_element_type=F32
            )
            for q in range(0, step, LANES):
                other = slice((1 - v) * half + i + q, (1 - v) * half + i + q + LANES)
                total = None
                for j in range(tiles):
                    k = (1 - v) * tiles + j
                    part = sink_ref[other, lane[j]] * scale_ref[k : k + 1, :] * s[q : q + LANES, lane[j]]
                    total = part if total is None else total + part
                r = (v * half + i + q) // LANES
                cross[pos, r : r + 1, :] = across_lanes(total)
    broadcast(CROSS, 2 * ny, pos, at_yc, cross)

    proto_result(0)
    crossz = rowz_buf.at[ITERS + 1]
    gathered(CROSS, 2 * ny, cross)
    crossz[z] = total_of(cross, 2 * ny)
    broadcast(CROSS + 1, ny, z, at_z, crossz)
    emb_result(0)
    proto_result(1)
    emb_result(1)

    gathered(CROSS + 1, ny, crossz)
    swapped = jnp.concatenate([weights[tiles:], weights[:tiles]], axis=0)
    loss = jnp.log(soft_total) - total_of(crossz, ny) * swapped
    for v in range(2):
        for j in range(tiles):
            loss_ref[v : v + 1, lane[j]] = loss[v * tiles + j : v * tiles + j + 1, :]

    for h in range(2):
        for d in reversed(far_first(ny)):
            j = lax.rem(ai + d, ny)
            block = ge_ref.at[pl.ds(c * half + (2 * j + h) * aq, aq)]
            pltpu.make_async_copy(block, block, block_sem.at[h, j]).wait()
            send(TO_SIBLING + h, block, block, sibling)
        sent(TO_SIBLING + h, ge_ref.at[pl.ds(0, step)])
    for h in range(2):
        arrived(PROTO_AG + h, gp_ref.at[pl.ds(0, (nx - 1) * xq)])
    flush()
    for h in range(2):
        arrived(TO_SIBLING + h, ge_ref.at[pl.ds(0, step)])


def finish(ge_ref, gp_ref, loss_ref, ge_out, gp_out, loss_out, sem):
    copies = [
        pltpu.make_async_copy(ge_ref, ge_out, sem.at[0]),
        pltpu.make_async_copy(gp_ref, gp_out, sem.at[1]),
        pltpu.make_async_copy(loss_ref, loss_out, sem.at[2]),
    ]
    for copy in copies:
        copy.start()
    for copy in copies:
        copy.wait()


def body(nx, ny, embeddings, prototypes):
    views, samples, width = embeddings.shape
    rows, cols = views * samples, prototypes.shape[0]
    aq, xq = samples // 2 // ny, cols // 2 // nx
    vmem = pl.BlockSpec(memory_space=pltpu.VMEM)
    hbm = pl.BlockSpec(memory_space=pltpu.HBM)
    shapes = (
        jax.ShapeDtypeStruct((rows, width), BF16),
        jax.ShapeDtypeStruct((cols, width), BF16),
        jax.ShapeDtypeStruct((views, samples), F32),
    )
    results = pl.pallas_call(
        functools.partial(kernel, nx, ny),
        out_shape=shapes,
        in_specs=[hbm, hbm],
        out_specs=(vmem, vmem, vmem),
        scratch_shapes=[
            pltpu.VMEM((rows, width), BF16),
            pltpu.VMEM((cols, width), BF16),
            pltpu.VMEM((rows, width), BF16),
            pltpu.VMEM((cols, width), BF16),
            pltpu.VMEM((rows, cols), F32),
            pltpu.VMEM((rows, cols), F32),
            pltpu.VMEM((rows, cols), BF16),
            pltpu.VMEM((ny, 2 * cols, width), BF16),
            pltpu.VMEM((ny, 2 * aq, 2 * cols), F32),
            pltpu.VMEM((ny, 2 * aq, 2 * cols), F32),
            pltpu.VMEM((ny, 2 * aq, 2 * cols), BF16),
            pltpu.VMEM((cols, width), F32),
            pltpu.VMEM((rows, LANES), F32),
            pltpu.VMEM((rows, LANES), F32),
            pltpu.VMEM((SUB, LANES), F32),
            pltpu.VMEM((ITERS, nx, SUB, LANES), F32),
            pltpu.VMEM((ITERS + 2, 2 * ny, SUB, LANES), F32),
            pltpu.VMEM((ITERS + 2, ny, SUB, LANES), F32),
            pltpu.VMEM((2 * ny, SUB, LANES), F32),
            pltpu.VMEM((2, ny, aq, width), F32),
            pltpu.VMEM((2, nx, xq, width), F32),
            pltpu.SemaphoreType.DMA((2,)),
            pltpu.SemaphoreType.DMA((STAGES,)),
            pltpu.SemaphoreType.DMA((STAGES,)),
            pltpu.SemaphoreType.DMA((ny,)),
            pltpu.SemaphoreType.DMA((2, ny)),
        ],
        compiler_params=pltpu.CompilerParams(
            collective_id=0, has_side_effects=True, vmem_limit_bytes=48 * 2**20
        ),
    )(
        pltpu.with_memory_space_constraint(embeddings.reshape(rows, width), pltpu.HBM),
        pltpu.with_memory_space_constraint(prototypes, pltpu.HBM),
    )
    ge, gp, loss = pl.pallas_call(
        finish,
        out_shape=shapes,
        in_specs=[vmem, vmem, vmem],
        out_specs=(hbm, hbm, hbm),
        scratch_shapes=[pltpu.SemaphoreType.DMA((3,))],
        compiler_params=pltpu.CompilerParams(vmem_limit_bytes=8 * 2**20),
    )(*results)
    return ge.reshape(views, samples, width), gp, loss


def solution(mesh):
    nx = mesh.shape["samp"]
    ny = 1
    while 2 * ny * ny < mesh.shape["proto"]:
        ny += 1
    return jax.shard_map(
        functools.partial(body, nx, ny),
        mesh=mesh,
        in_specs=(P(None, "samp", None), P("proto", None)),
        out_specs=(P(None, "samp", None), P("proto", None), P(None, "samp")),
        check_vma=False,
    )
```

```python
import functools

import jax
import jax.numpy as jnp
from jax import lax
from jax.experimental import pallas as pl
from jax.experimental.pallas import tpu as pltpu
from jax.sharding import PartitionSpec as P

ITERS = 3
INV_TEMPER = 10.0
F32 = jnp.float32
BF16 = jnp.bfloat16
MESH = pl.DeviceIdType.MESH
LANES = 128
SUB = 8
SOFT = 9
PROTO_RS = 11
PROTO_AG = 13
EMB_B = 15
EMB_AG = 17
TO_SIBLING = 19
CROSS = 21
SCALES = 23
PAIR = 24
RING = 25
STAGES = 29


def normalize_rows(values):
    as_float = values.astype(F32)
    inverse = lax.rsqrt(jnp.sum(as_float * as_float, axis=-1, keepdims=True) + 1e-06)
    return as_float * inverse, inverse


def project(summed, unit_rows, inverse):
    return (summed - unit_rows * jnp.sum(unit_rows * summed, axis=-1, keepdims=True)) * inverse


def far_first(count):
    half = count // 2
    order = [half]
    for step in range(1, half + 1):
        for offset in (half - step, half + step):
            if 0 < offset < count and offset not in order:
                order.append(offset)
    return order


def kernel(
    nx,
    ny,
    emb_hbm,
    proto_hbm,
    ge_ref,
    gp_ref,
    loss_ref,
    emb_ref,
    proto_ref,
    eb_ref,
    pb_ref,
    soft_ref,
    sink_ref,
    slope_ref,
    ring_ref,
    ring_soft,
    ring_sink,
    ring_slope,
    ppart_ref,
    wcol_ref,
    tcol_ref,
    scale_ref,
    col_buf,
    row_buf,
    rowz_buf,
    scales_buf,
    b_buf,
    x_buf,
    load_sem,
    send_sem,
    recv_sem,
    ring_sem,
    block_sem,
):
    rows, width = eb_ref.shape
    half = rows // 2
    cols = pb_ref.shape[0]
    tiles = cols // LANES
    x = lax.axis_index("samp")
    p = lax.axis_index("proto")
    y = p // (2 * ny)
    z = (p // 2) % ny
    c = p % 2
    pos = y * 2 + c
    ai = y + (z - y) * c
    bi = z + (y - z) * c
    astep = 2 * ny + (2 - 2 * ny) * c
    bstep = 2 + (2 * ny - 2) * c
    step = half // 2
    xstep = cols // 2
    aq = step // ny
    xq = xstep // nx

    def at_x(j):
        return (j, p)

    def at_yc(j):
        return (x, (j // 2) * (2 * ny) + z * 2 + j % 2)

    def at_z(j):
        return (x, y * (2 * ny) + j * 2 + c)

    def at_a(j):
        return (x, p + (j - ai) * astep)

    def at_b(j):
        return (x, p + (j - bi) * bstep)

    sibling = (x, p + 1 - 2 * c)

    load_proto = pltpu.make_async_copy(proto_hbm, proto_ref, load_sem.at[0])
    load_emb = pltpu.make_async_copy(emb_hbm, emb_ref, load_sem.at[1])
    load_proto.start()
    load_emb.start()

    barrier = pltpu.get_barrier_semaphore()

    def greet(device):
        pl.semaphore_signal(barrier, inc=1, device_id=device, device_id_type=MESH)

    for d in far_first(nx):
        greet(at_x(lax.rem(x + d, nx)))
    for d in far_first(ny):
        for core in range(2):
            greet((x, lax.rem(y + d, ny) * (2 * ny) + z * 2 + core))
            greet((x, y * (2 * ny) + lax.rem(z + d, ny) * 2 + core))
    greet(sibling)
    greetings = nx - 1 + 4 * (ny - 1) + 1

    pending = []

    def sent(stage, ref):
        pending.append(pltpu.make_async_copy(ref, ref, send_sem.at[stage]))

    def flush():
        for copy in pending:
            copy.wait()
        pending.clear()

    def send(stage, source, place, device, received=None):
        pltpu.make_async_remote_copy(
            src_ref=source,
            dst_ref=place,
            send_sem=send_sem.at[stage],
            recv_sem=recv_sem.at[stage] if received is None else received,
            device_id=device,
            device_id_type=MESH,
        ).start()

    def broadcast(stage, count, me, at, buf):
        for d in far_first(count):
            send(stage, buf.at[me], buf.at[me], at(lax.rem(me + d, count)))
        sent(stage, buf.at[pl.ds(0, count - 1)])

    def arrived(stage, ref):
        pltpu.make_async_copy(ref, ref, recv_sem.at[stage]).wait()

    def gathered(stage, count, buf):
        arrived(stage, buf.at[pl.ds(0, count - 1)])

    def total_of(ref, count):
        total = ref[0]
        for j in range(1, count):
            total = total + ref[j]
        return total

    def fold(block):
        return jnp.sum(block.reshape(-1, SUB, LANES), axis=0)

    def across_lanes(block):
        return jnp.sum(fold(block.T), axis=0, keepdims=True)

    def store_columns(ref, tile):
        for r in range(SUB):
            ref[r * LANES : (r + 1) * LANES, :] = jnp.broadcast_to(tile[r : r + 1, :], (LANES, LANES)).T

    lane = [slice(j * LANES, (j + 1) * LANES) for j in range(tiles)]

    load_proto.wait()
    unit_proto, _ = normalize_rows(proto_ref[...])
    pb_ref[...] = unit_proto.astype(BF16)
    ring_ref[ai, pl.ds(pl.multiple_of(c * cols, cols), cols), :] = pb_ref[...]
    load_emb.wait()
    col = col_buf.at[0]
    for v in range(2):
        sums = [None] * tiles
        for i in range(v * half, (v + 1) * half, step):
            unit, _ = normalize_rows(emb_ref[i : i + step, :])
            eb = unit.astype(BF16)
            eb_ref[i : i + step, :] = eb
            s = lax.dot_general(eb, pb_ref[...], (((1,), (1,)), ((), ())), preferred_element_type=F32)
            soft = jnp.exp(s * INV_TEMPER)
            soft_ref[i : i + step, :] = soft
            for j in range(tiles):
                part = fold(soft[:, lane[j]] * soft[:, lane[j]])
                sums[j] = part if sums[j] is None else sums[j] + part
        for j in range(tiles):
            k = v * tiles + j
            col[x, k : k + 1, :] = jnp.sum(sums[j], axis=0, keepdims=True)

    pl.semaphore_wait(barrier, greetings)

    right = lax.rem(ai + 1, ny)
    left = lax.rem(ai + ny - 1, ny)

    def slot(offset):
        return lax.rem(ai + offset + ny, ny)

    def pass_on(hop):
        back, ahead = slot(-hop), slot(hop)
        if hop < ny // 2 - 1:
            send(RING + hop, ring_ref.at[back], ring_ref.at[back], at_a(right), ring_sem.at[back])
            send(RING + hop, ring_ref.at[ahead], ring_ref.at[ahead], at_a(left), ring_sem.at[ahead])
            sent(RING + hop, ring_ref.at[pl.ds(0, 2)])
        else:
            for to, origin, half_of in ((right, back, 0), (left, ahead, 1)):
                block = ring_ref.at[origin, pl.ds(half_of * cols, cols)]
                send(RING + hop, block, block, at_a(to), ring_sem.at[origin])
            sent(RING + hop, ring_ref.at[0])

    def passed(offset):
        block = ring_ref.at[slot(offset)]
        pltpu.make_async_copy(block, block, ring_sem.at[slot(offset)]).wait()

    def ring_share():
        return tcol_ref[pl.ds(pl.multiple_of(c * half + ai * 2 * aq, 2 * aq), 2 * aq), :]

    def ring_terms(offset):
        mine = eb_ref[pl.ds(pl.multiple_of(c * half + ai * 2 * aq, 2 * aq), 2 * aq), :]
        other = eb_ref[pl.ds(pl.multiple_of((1 - c) * half + ai * 2 * aq, 2 * aq), 2 * aq), :]
        both = jnp.concatenate([mine, other], axis=0)
        for k in range(0, 2 * cols, cols):
            s = lax.dot_general(
                both,
                ring_ref[slot(offset), k : k + cols, :],
                (((1,), (1,)), ((), ())),
                preferred_element_type=F32,
            )
            soft = jnp.exp(s * INV_TEMPER)
            mine_soft = soft[: 2 * aq]
            if abs(offset) > 1:
                mine_soft = mine_soft * jnp.concatenate([ring_share()] * tiles, axis=1)
            ring_soft[offset % ny, :, k : k + cols] = mine_soft
            ring_sink[offset % ny, :, k : k + cols] = soft[2 * aq :] * soft[2 * aq :]

    def row_sums(buf, scale):
        for r in range(SUB):
            v = r // tiles
            block = slice(r * LANES, (r + 1) * LANES)
            total = None
            for j in range(tiles):
                k = v * tiles + j
                part = sink_ref[block, lane[j]] * scale[k : k + 1, :]
                total = part if total is None else total + part
            buf[pos, r : r + 1, :] = across_lanes(total)

    soft_total = None
    weights = None
    scale = None
    extra = row_buf.at[ITERS]
    extraz = rowz_buf.at[ITERS]
    for sweep in range(ITERS):
        col = col_buf.at[sweep]
        if sweep > 0:
            for v in range(2):
                sums = [None] * tiles
                for i in range(v * half, (v + 1) * half, 64):
                    weight = wcol_ref[i : i + 64, :]
                    for j in range(tiles):
                        part = fold(sink_ref[i : i + 64, lane[j]] * weight)
                        sums[j] = part if sums[j] is None else sums[j] + part
                for j in range(tiles):
                    k = v * tiles + j
                    col[x, k : k + 1, :] = jnp.sum(sums[j], axis=0, keepdims=True)
        stage = 3 * sweep
        broadcast(stage, nx, x, at_x, col)
        if sweep == 0:
            pair = ring_ref.at[ai, pl.ds(c * cols, cols)]
            send(PAIR, pair, ring_ref.at[bi, pl.ds(c * cols, cols)], sibling)
            sent(PAIR, pb_ref)
        if sweep == 1:
            ring_terms(1)
            ring_terms(-1)
        if sweep == 2:
            passed(3)
            passed(-3)
            pass_on(3)
            ring_terms(3)
            ring_terms(-3)
        if sweep == 0:
            for r in range(SUB):
                block = slice(r * LANES, (r + 1) * LANES)
                total = None
                for j in range(tiles):
                    soft = soft_ref[block, lane[j]]
                    sink_ref[block, lane[j]] = soft * soft
                    total = soft if total is None else total + soft
                extra[pos, r : r + 1, :] = across_lanes(total)
            broadcast(SOFT, 2 * ny, pos, at_yc, extra)
            arrived(PAIR, pb_ref)
            pass_on(0)
        gathered(stage, nx, col)
        scale = 1.0 / total_of(col, nx)
        row = row_buf.at[sweep]
        row_sums(row, scale)
        broadcast(stage + 1, 2 * ny, pos, at_yc, row)
        if sweep == 0:
            gathered(SOFT, 2 * ny, extra)
            extraz[z] = total_of(extra, 2 * ny)
            broadcast(SOFT + 1, ny, z, at_z, extraz)
            ring_terms(0)
        if sweep == 1:
            passed(2)
            passed(-2)
            pass_on(2)
        if sweep == 2:
            tens = scale * INV_TEMPER
            scale_ref[...] = tens
            scales_buf[ai * 2 + c] = tens
            for d in far_first(ny):
                send(SCALES, scale_ref, scales_buf.at[y * 2 + c], (x, lax.rem(y + d, ny) * (2 * ny) + z * 2))
                send(SCALES, scale_ref, scales_buf.at[z * 2 + c], (x, y * (2 * ny) + lax.rem(z + d, ny) * 2 + 1))
            send(SCALES, scale_ref, scales_buf.at[bi * 2 + c], sibling)
            sent(SCALES, scales_buf.at[pl.ds(0, 2 * ny - 1)])
            for r in range(SUB):
                block = slice(r * LANES, (r + 1) * LANES)
                for j in range(tiles):
                    k = r // tiles * tiles + j
                    sink_ref[block, lane[j]] = sink_ref[block, lane[j]] * tens[k : k + 1, :]
        gathered(stage + 1, 2 * ny, row)
        rowz = rowz_buf.at[sweep]
        rowz[z] = total_of(row, 2 * ny)
        broadcast(stage + 2, ny, z, at_z, rowz)
        if sweep == 1:
            gathered(SOFT + 1, ny, extraz)
            soft_total = total_of(extraz, ny)
            store_columns(tcol_ref, INV_TEMPER / soft_total)
            for i in range(0, rows, LANES):
                share = tcol_ref[i : i + LANES, :]
                for j in range(tiles):
                    soft_ref[i : i + LANES, lane[j]] = soft_ref[i : i + LANES, lane[j]] * share
            share = ring_share()
            for offset in (0, 1, ny - 1):
                for k in range(2 * tiles):
                    at = slice(k * LANES, (k + 1) * LANES)
                    ring_soft[offset, :, at] = ring_soft[offset, :, at] * share
            ring_terms(2)
            ring_terms(-2)
        if sweep == 0:
            passed(1)
            passed(-1)
            pass_on(1)
        if sweep == 2:
            passed(4)
            ring_terms(4)
            gathered(SCALES, 2 * ny, scales_buf)
            for offset in range(ny):
                for k in range(2 * tiles):
                    at = slice(k * LANES, (k + 1) * LANES)
                    factor = scales_buf[slot(offset) * 2 + k // tiles, pl.ds((1 - c) * tiles + k % tiles, 1), :]
                    ring_sink[offset, :, at] = ring_sink[offset, :, at] * factor
            flush()
        gathered(stage + 2, ny, rowz)
        weights = 1.0 / total_of(rowz, ny)
        store_columns(wcol_ref, weights)

    def slopes(v, h):
        mine = v * half + h * step
        other = (1 - v) * half + h * step
        for i in range(0, step, LANES):
            here = pl.ds(mine + i, LANES)
            there = pl.ds(other + i, LANES)
            weight = wcol_ref[there, :]
            for j in range(tiles):
                slope_ref[here, lane[j]] = (soft_ref[here, lane[j]] - sink_ref[there, lane[j]] * weight).astype(BF16)

    def proto_terms(h):
        for k in range(h * xstep, (h + 1) * xstep, LANES):
            ppart_ref[k : k + LANES, :] = lax.dot_general(
                slope_ref[:, k : k + LANES], eb_ref[...], (((0,), (0,)), ((), ())), preferred_element_type=F32
            )
        for d in far_first(nx):
            j = lax.rem(x + d, nx)
            send(PROTO_RS + h, ppart_ref.at[pl.ds(h * xstep + j * xq, xq)], x_buf.at[h, x], at_x(j))
        sent(PROTO_RS + h, x_buf.at[h, pl.ds(0, nx - 1)])
        x_buf[h, x] = ppart_ref[pl.ds(h * xstep + x * xq, xq), :]

    def proto_result(h):
        own = pl.ds(h * xstep + x * xq, xq)
        unit, inverse = normalize_rows(proto_ref[own, :])
        gathered(PROTO_RS + h, nx, x_buf.at[h])
        gp_ref[own, :] = project(total_of(x_buf.at[h], nx), unit, inverse).astype(BF16)
        for d in far_first(nx):
            send(PROTO_AG + h, gp_ref.at[own], gp_ref.at[own], at_x(lax.rem(x + d, nx)))
        sent(PROTO_AG + h, gp_ref.at[pl.ds(0, (nx - 1) * xq)])

    def emb_result(h):
        own = pl.ds(c * half + (2 * ai + h) * aq, aq)
        unit, inverse = normalize_rows(emb_ref[own, :])
        gathered(EMB_B + h, ny, b_buf.at[h])
        ge_ref[own, :] = project(total_of(b_buf.at[h], ny), unit, inverse).astype(BF16)
        block = ge_ref.at[own]
        for d in far_first(ny):
            send(EMB_AG + h, block, block, at_a(lax.rem(ai + d, ny)), block_sem.at[h, ai])
        sent(EMB_AG + h, ge_ref.at[pl.ds(0, (ny - 1) * aq)])
        send(TO_SIBLING + h, block, block, sibling)

    for v in range(2):
        for h in range(2):
            slopes(v, h)
    proto_terms(0)
    weight = wcol_ref[pl.ds(pl.multiple_of((1 - c) * half + ai * 2 * aq, 2 * aq), 2 * aq), :]
    total = None
    for offset in range(ny):
        for k in range(2 * tiles):
            at = slice(k * LANES, (k + 1) * LANES)
            ring_slope[offset, :, at] = (ring_soft[offset, :, at] - ring_sink[offset, :, at] * weight).astype(BF16)
        part = jnp.dot(ring_slope[offset], ring_ref[slot(offset)], preferred_element_type=F32)
        total = part if total is None else total + part
    for h in range(2):
        b_buf[h, bi] = total[h * aq : (h + 1) * aq]
        broadcast(EMB_B + h, ny, bi, at_b, b_buf.at[h])
    proto_terms(1)

    cross = row_buf.at[ITERS + 1]
    for v in range(2):
        for i in range(0, half, step):
            here = slice(v * half + i, v * half + i + step)
            s = lax.dot_general(
                eb_ref[here, :], pb_ref[...], (((1,), (1,)), ((), ())), preferred_element_type=F32
            )
            for q in range(0, step, LANES):
                other = slice((1 - v) * half + i + q, (1 - v) * half + i + q + LANES)
                total = None
                for j in range(tiles):
                    part = sink_ref[other, lane[j]] * s[q : q + LANES, lane[j]]
                    total = part if total is None else total + part
                r = (v * half + i + q) // LANES
                cross[pos, r : r + 1, :] = across_lanes(total)
    broadcast(CROSS, 2 * ny, pos, at_yc, cross)

    proto_result(0)
    crossz = rowz_buf.at[ITERS + 1]
    gathered(CROSS, 2 * ny, cross)
    crossz[z] = total_of(cross, 2 * ny)
    broadcast(CROSS + 1, ny, z, at_z, crossz)
    emb_result(0)
    proto_result(1)
    emb_result(1)

    gathered(CROSS + 1, ny, crossz)
    swapped = jnp.concatenate([weights[tiles:], weights[:tiles]], axis=0)
    loss = jnp.log(soft_total) - total_of(crossz, ny) * swapped
    for v in range(2):
        for j in range(tiles):
            loss_ref[v : v + 1, lane[j]] = loss[v * tiles + j : v * tiles + j + 1, :]

    for h in range(2):
        for d in reversed(far_first(ny)):
            j = lax.rem(ai + d, ny)
            block = ge_ref.at[pl.ds(c * half + (2 * j + h) * aq, aq)]
            pltpu.make_async_copy(block, block, block_sem.at[h, j]).wait()
            send(TO_SIBLING + h, block, block, sibling)
        sent(TO_SIBLING + h, ge_ref.at[pl.ds(0, step)])
    for h in range(2):
        arrived(PROTO_AG + h, gp_ref.at[pl.ds(0, (nx - 1) * xq)])
    flush()
    for h in range(2):
        arrived(TO_SIBLING + h, ge_ref.at[pl.ds(0, step)])


def finish(ge_ref, gp_ref, loss_ref, ge_out, gp_out, loss_out, sem):
    copies = [
        pltpu.make_async_copy(ge_ref, ge_out, sem.at[0]),
        pltpu.make_async_copy(gp_ref, gp_out, sem.at[1]),
        pltpu.make_async_copy(loss_ref, loss_out, sem.at[2]),
    ]
    for copy in copies:
        copy.start()
    for copy in copies:
        copy.wait()


def body(nx, ny, embeddings, prototypes):
    views, samples, width = embeddings.shape
    rows, cols = views * samples, prototypes.shape[0]
    aq, xq = samples // 2 // ny, cols // 2 // nx
    vmem = pl.BlockSpec(memory_space=pltpu.VMEM)
    hbm = pl.BlockSpec(memory_space=pltpu.HBM)
    shapes = (
        jax.ShapeDtypeStruct((rows, width), BF16),
        jax.ShapeDtypeStruct((cols, width), BF16),
        jax.ShapeDtypeStruct((views, samples), F32),
    )
    results = pl.pallas_call(
        functools.partial(kernel, nx, ny),
        out_shape=shapes,
        in_specs=[hbm, hbm],
        out_specs=(vmem, vmem, vmem),
        scratch_shapes=[
            pltpu.VMEM((rows, width), BF16),
            pltpu.VMEM((cols, width), BF16),
            pltpu.VMEM((rows, width), BF16),
            pltpu.VMEM((cols, width), BF16),
            pltpu.VMEM((rows, cols), F32),
            pltpu.VMEM((rows, cols), F32),
            pltpu.VMEM((rows, cols), BF16),
            pltpu.VMEM((ny, 2 * cols, width), BF16),
            pltpu.VMEM((ny, 2 * aq, 2 * cols), F32),
            pltpu.VMEM((ny, 2 * aq, 2 * cols), F32),
            pltpu.VMEM((ny, 2 * aq, 2 * cols), BF16),
            pltpu.VMEM((cols, width), F32),
            pltpu.VMEM((rows, LANES), F32),
            pltpu.VMEM((rows, LANES), F32),
            pltpu.VMEM((SUB, LANES), F32),
            pltpu.VMEM((ITERS, nx, SUB, LANES), F32),
            pltpu.VMEM((ITERS + 2, 2 * ny, SUB, LANES), F32),
            pltpu.VMEM((ITERS + 2, ny, SUB, LANES), F32),
            pltpu.VMEM((2 * ny, SUB, LANES), F32),
            pltpu.VMEM((2, ny, aq, width), F32),
            pltpu.VMEM((2, nx, xq, width), F32),
            pltpu.SemaphoreType.DMA((2,)),
            pltpu.SemaphoreType.DMA((STAGES,)),
            pltpu.SemaphoreType.DMA((STAGES,)),
            pltpu.SemaphoreType.DMA((ny,)),
            pltpu.SemaphoreType.DMA((2, ny)),
        ],
        compiler_params=pltpu.CompilerParams(
            collective_id=0, has_side_effects=True, vmem_limit_bytes=48 * 2**20
        ),
    )(
        pltpu.with_memory_space_constraint(embeddings.reshape(rows, width), pltpu.HBM),
        pltpu.with_memory_space_constraint(prototypes, pltpu.HBM),
    )
    ge, gp, loss = pl.pallas_call(
        finish,
        out_shape=shapes,
        in_specs=[vmem, vmem, vmem],
        out_specs=(hbm, hbm, hbm),
        scratch_shapes=[pltpu.SemaphoreType.DMA((3,))],
        compiler_params=pltpu.CompilerParams(vmem_limit_bytes=8 * 2**20),
    )(*results)
    return ge.reshape(views, samples, width), gp, loss


def solution(mesh):
    nx = mesh.shape["samp"]
    ny = 1
    while 2 * ny * ny < mesh.shape["proto"]:
        ny += 1
    return jax.shard_map(
        functools.partial(body, nx, ny),
        mesh=mesh,
        in_specs=(P(None, "samp", None), P("proto", None)),
        out_specs=(P(None, "samp", None), P("proto", None), P(None, "samp")),
        check_vma=False,
    )
```

```python
import functools

import jax
import jax.numpy as jnp
from jax import lax
from jax.experimental import pallas as pl
from jax.experimental.pallas import tpu as pltpu
from jax.sharding import PartitionSpec as P

ITERS = 3
INV_TEMPER = 10.0
F32 = jnp.float32
BF16 = jnp.bfloat16
MESH = pl.DeviceIdType.MESH
LANES = 128
SUB = 8
SOFT = 9
PROTO_RS = 11
PROTO_AG = 13
EMB_B = 15
EMB_AG = 17
TO_SIBLING = 19
CROSS = 21
SCALES = 23
PAIR = 24
RING = 25
STAGES = 29


def normalize_rows(values):
    as_float = values.astype(F32)
    inverse = lax.rsqrt(jnp.sum(as_float * as_float, axis=-1, keepdims=True) + 1e-06)
    return as_float * inverse, inverse


def project(summed, unit_rows, inverse):
    return (summed - unit_rows * jnp.sum(unit_rows * summed, axis=-1, keepdims=True)) * inverse


def far_first(count):
    half = count // 2
    order = [half]
    for step in range(1, half + 1):
        for offset in (half - step, half + step):
            if 0 < offset < count and offset not in order:
                order.append(offset)
    return order


def kernel(
    nx,
    ny,
    emb_hbm,
    proto_hbm,
    ge_ref,
    gp_ref,
    loss_ref,
    emb_ref,
    proto_ref,
    eb_ref,
    pb_ref,
    soft_ref,
    sink_ref,
    slope_ref,
    ring_ref,
    ring_soft,
    ring_sink,
    ring_slope,
    ppart_ref,
    wcol_ref,
    tcol_ref,
    scale_ref,
    col_buf,
    row_buf,
    rowz_buf,
    scales_buf,
    b_buf,
    x_buf,
    load_sem,
    send_sem,
    recv_sem,
    ring_sem,
    block_sem,
):
    rows, width = eb_ref.shape
    half = rows // 2
    cols = pb_ref.shape[0]
    tiles = cols // LANES
    x = lax.axis_index("samp")
    p = lax.axis_index("proto")
    y = p // (2 * ny)
    z = (p // 2) % ny
    c = p % 2
    pos = y * 2 + c
    ai = y + (z - y) * c
    bi = z + (y - z) * c
    astep = 2 * ny + (2 - 2 * ny) * c
    bstep = 2 + (2 * ny - 2) * c
    step = half // 2
    xstep = cols // 2
    aq = step // ny
    xq = xstep // nx

    def at_x(j):
        return (j, p)

    def at_yc(j):
        return (x, (j // 2) * (2 * ny) + z * 2 + j % 2)

    def at_z(j):
        return (x, y * (2 * ny) + j * 2 + c)

    def at_a(j):
        return (x, p + (j - ai) * astep)

    def at_b(j):
        return (x, p + (j - bi) * bstep)

    sibling = (x, p + 1 - 2 * c)

    load_proto = pltpu.make_async_copy(proto_hbm, proto_ref, load_sem.at[0])
    load_emb = pltpu.make_async_copy(emb_hbm, emb_ref, load_sem.at[1])
    load_proto.start()
    load_emb.start()

    barrier = pltpu.get_barrier_semaphore()

    def greet(device):
        pl.semaphore_signal(barrier, inc=1, device_id=device, device_id_type=MESH)

    for d in far_first(nx):
        greet(at_x(lax.rem(x + d, nx)))
    for d in far_first(ny):
        for core in range(2):
            greet((x, lax.rem(y + d, ny) * (2 * ny) + z * 2 + core))
            greet((x, y * (2 * ny) + lax.rem(z + d, ny) * 2 + core))
    greet(sibling)
    greetings = nx - 1 + 4 * (ny - 1) + 1

    pending = []

    def sent(stage, ref):
        pending.append(pltpu.make_async_copy(ref, ref, send_sem.at[stage]))

    def flush():
        for copy in pending:
            copy.wait()
        pending.clear()

    def send(stage, source, place, device, received=None):
        pltpu.make_async_remote_copy(
            src_ref=source,
            dst_ref=place,
            send_sem=send_sem.at[stage],
            recv_sem=recv_sem.at[stage] if received is None else received,
            device_id=device,
            device_id_type=MESH,
        ).start()

    def broadcast(stage, count, me, at, buf):
        for d in far_first(count):
            send(stage, buf.at[me], buf.at[me], at(lax.rem(me + d, count)))
        sent(stage, buf.at[pl.ds(0, count - 1)])

    def arrived(stage, ref):
        pltpu.make_async_copy(ref, ref, recv_sem.at[stage]).wait()

    def gathered(stage, count, buf):
        arrived(stage, buf.at[pl.ds(0, count - 1)])

    def total_of(ref, count):
        total = ref[0]
        for j in range(1, count):
            total = total + ref[j]
        return total

    def fold(block):
        return jnp.sum(block.reshape(-1, SUB, LANES), axis=0)

    def across_lanes(block):
        return jnp.sum(fold(block.T), axis=0, keepdims=True)

    def store_columns(ref, tile):
        for r in range(SUB):
            ref[r * LANES : (r + 1) * LANES, :] = jnp.broadcast_to(tile[r : r + 1, :], (LANES, LANES)).T

    lane = [slice(j * LANES, (j + 1) * LANES) for j in range(tiles)]

    load_proto.wait()
    unit_proto, _ = normalize_rows(proto_ref[...])
    pb_ref[...] = unit_proto.astype(BF16)
    ring_ref[ai, pl.ds(pl.multiple_of(c * cols, cols), cols), :] = pb_ref[...]
    load_emb.wait()
    col = col_buf.at[0]
    for v in range(2):
        sums = [None] * tiles
        for i in range(v * half, (v + 1) * half, step):
            unit, _ = normalize_rows(emb_ref[i : i + step, :])
            eb = unit.astype(BF16)
            eb_ref[i : i + step, :] = eb
            s = lax.dot_general(eb, pb_ref[...], (((1,), (1,)), ((), ())), preferred_element_type=F32)
            soft = jnp.exp(s * INV_TEMPER)
            soft_ref[i : i + step, :] = soft
            for j in range(tiles):
                part = fold(soft[:, lane[j]] * soft[:, lane[j]])
                sums[j] = part if sums[j] is None else sums[j] + part
        for j in range(tiles):
            k = v * tiles + j
            col[x, k : k + 1, :] = jnp.sum(sums[j], axis=0, keepdims=True)

    pl.semaphore_wait(barrier, greetings)

    right = lax.rem(ai + 1, ny)
    left = lax.rem(ai + ny - 1, ny)

    def slot(offset):
        return lax.rem(ai + offset + ny, ny)

    def pass_on(hop):
        back, ahead = slot(-hop), slot(hop)
        if hop < ny // 2 - 1:
            send(RING + hop, ring_ref.at[back], ring_ref.at[back], at_a(right), ring_sem.at[back])
            send(RING + hop, ring_ref.at[ahead], ring_ref.at[ahead], at_a(left), ring_sem.at[ahead])
            sent(RING + hop, ring_ref.at[pl.ds(0, 2)])
        else:
            for to, origin, half_of in ((right, back, 0), (left, ahead, 1)):
                block = ring_ref.at[origin, pl.ds(half_of * cols, cols)]
                send(RING + hop, block, block, at_a(to), ring_sem.at[origin])
            sent(RING + hop, ring_ref.at[0])

    def passed(offset):
        block = ring_ref.at[slot(offset)]
        pltpu.make_async_copy(block, block, ring_sem.at[slot(offset)]).wait()

    def ring_share():
        return tcol_ref[pl.ds(pl.multiple_of(c * half + ai * 2 * aq, 2 * aq), 2 * aq), :]

    def ring_terms(offset):
        mine = eb_ref[pl.ds(pl.multiple_of(c * half + ai * 2 * aq, 2 * aq), 2 * aq), :]
        other = eb_ref[pl.ds(pl.multiple_of((1 - c) * half + ai * 2 * aq, 2 * aq), 2 * aq), :]
        both = jnp.concatenate([mine, other], axis=0)
        for k in range(0, 2 * cols, cols):
            s = lax.dot_general(
                both,
                ring_ref[slot(offset), k : k + cols, :],
                (((1,), (1,)), ((), ())),
                preferred_element_type=F32,
            )
            soft = jnp.exp(s * INV_TEMPER)
            mine_soft = soft[: 2 * aq]
            if abs(offset) > 1:
                mine_soft = mine_soft * jnp.concatenate([ring_share()] * tiles, axis=1)
            ring_soft[offset % ny, :, k : k + cols] = mine_soft
            ring_sink[offset % ny, :, k : k + cols] = soft[2 * aq :] * soft[2 * aq :]

    def row_sums(buf, scale):
        for r in range(SUB):
            v = r // tiles
            block = slice(r * LANES, (r + 1) * LANES)
            total = None
            for j in range(tiles):
                k = v * tiles + j
                part = sink_ref[block, lane[j]] * scale[k : k + 1, :]
                total = part if total is None else total + part
            buf[pos, r : r + 1, :] = across_lanes(total)

    soft_total = None
    weights = None
    scale = None
    extra = row_buf.at[ITERS]
    extraz = rowz_buf.at[ITERS]
    for sweep in range(ITERS):
        col = col_buf.at[sweep]
        if sweep > 0:
            for v in range(2):
                sums = [None] * tiles
                for i in range(v * half, (v + 1) * half, 64):
                    weight = wcol_ref[i : i + 64, :]
                    for j in range(tiles):
                        part = fold(sink_ref[i : i + 64, lane[j]] * weight)
                        sums[j] = part if sums[j] is None else sums[j] + part
                for j in range(tiles):
                    k = v * tiles + j
                    col[x, k : k + 1, :] = jnp.sum(sums[j], axis=0, keepdims=True)
        stage = 3 * sweep
        broadcast(stage, nx, x, at_x, col)
        if sweep == 0:
            pair = ring_ref.at[ai, pl.ds(c * cols, cols)]
            send(PAIR, pair, ring_ref.at[bi, pl.ds(c * cols, cols)], sibling)
            sent(PAIR, pb_ref)
        if sweep == 1:
            ring_terms(1)
            ring_terms(-1)
        if sweep == 2:
            passed(3)
            passed(-3)
            pass_on(3)
            ring_terms(3)
            ring_terms(-3)
        if sweep == 0:
            for r in range(SUB):
                block = slice(r * LANES, (r + 1) * LANES)
                total = None
                for j in range(tiles):
                    soft = soft_ref[block, lane[j]]
                    sink_ref[block, lane[j]] = soft * soft
                    total = soft if total is None else total + soft
                extra[pos, r : r + 1, :] = across_lanes(total)
            broadcast(SOFT, 2 * ny, pos, at_yc, extra)
            arrived(PAIR, pb_ref)
            pass_on(0)
        gathered(stage, nx, col)
        scale = 1.0 / total_of(col, nx)
        row = row_buf.at[sweep]
        row_sums(row, scale)
        broadcast(stage + 1, 2 * ny, pos, at_yc, row)
        if sweep == 0:
            gathered(SOFT, 2 * ny, extra)
            extraz[z] = total_of(extra, 2 * ny)
            broadcast(SOFT + 1, ny, z, at_z, extraz)
            ring_terms(0)
        if sweep == 1:
            passed(2)
            passed(-2)
            pass_on(2)
        if sweep == 2:
            tens = scale * INV_TEMPER
            scale_ref[...] = tens
            scales_buf[ai * 2 + c] = tens
            for d in far_first(ny):
                send(SCALES, scale_ref, scales_buf.at[y * 2 + c], (x, lax.rem(y + d, ny) * (2 * ny) + z * 2))
                send(SCALES, scale_ref, scales_buf.at[z * 2 + c], (x, y * (2 * ny) + lax.rem(z + d, ny) * 2 + 1))
            send(SCALES, scale_ref, scales_buf.at[bi * 2 + c], sibling)
            sent(SCALES, scales_buf.at[pl.ds(0, 2 * ny - 1)])
            for r in range(SUB):
                block = slice(r * LANES, (r + 1) * LANES)
                for j in range(tiles):
                    k = r // tiles * tiles + j
                    sink_ref[block, lane[j]] = sink_ref[block, lane[j]] * tens[k : k + 1, :]
        gathered(stage + 1, 2 * ny, row)
        rowz = rowz_buf.at[sweep]
        rowz[z] = total_of(row, 2 * ny)
        broadcast(stage + 2, ny, z, at_z, rowz)
        if sweep == 1:
            gathered(SOFT + 1, ny, extraz)
            soft_total = total_of(extraz, ny)
            store_columns(tcol_ref, INV_TEMPER / soft_total)
            for i in range(0, rows, LANES):
                share = tcol_ref[i : i + LANES, :]
                for j in range(tiles):
                    soft_ref[i : i + LANES, lane[j]] = soft_ref[i : i + LANES, lane[j]] * share
            share = ring_share()
            for offset in (0, 1, ny - 1):
                for k in range(2 * tiles):
                    at = slice(k * LANES, (k + 1) * LANES)
                    ring_soft[offset, :, at] = ring_soft[offset, :, at] * share
            ring_terms(2)
            ring_terms(-2)
        if sweep == 0:
            passed(1)
            passed(-1)
            pass_on(1)
        if sweep == 2:
            passed(4)
            ring_terms(4)
            gathered(SCALES, 2 * ny, scales_buf)
            for offset in range(ny):
                for k in range(2 * tiles):
                    at = slice(k * LANES, (k + 1) * LANES)
                    factor = scales_buf[slot(offset) * 2 + k // tiles, pl.ds((1 - c) * tiles + k % tiles, 1), :]
                    ring_sink[offset, :, at] = ring_sink[offset, :, at] * factor
            flush()
        gathered(stage + 2, ny, rowz)
        weights = 1.0 / total_of(rowz, ny)
        store_columns(wcol_ref, weights)

    def slopes(v, h):
        mine = v * half + h * step
        other = (1 - v) * half + h * step
        for i in range(0, step, LANES):
            here = pl.ds(mine + i, LANES)
            there = pl.ds(other + i, LANES)
            weight = wcol_ref[there, :]
            for j in range(tiles):
                slope_ref[here, lane[j]] = (soft_ref[here, lane[j]] - sink_ref[there, lane[j]] * weight).astype(BF16)

    def proto_terms(h):
        for k in range(h * xstep, (h + 1) * xstep, LANES):
            ppart_ref[k : k + LANES, :] = lax.dot_general(
                slope_ref[:, k : k + LANES], eb_ref[...], (((0,), (0,)), ((), ())), preferred_element_type=F32
            )
        for d in far_first(nx):
            j = lax.rem(x + d, nx)
            send(PROTO_RS + h, ppart_ref.at[pl.ds(h * xstep + j * xq, xq)], x_buf.at[h, x], at_x(j))
        sent(PROTO_RS + h, x_buf.at[h, pl.ds(0, nx - 1)])
        x_buf[h, x] = ppart_ref[pl.ds(h * xstep + x * xq, xq), :]

    def proto_result(h):
        own = pl.ds(h * xstep + x * xq, xq)
        unit, inverse = normalize_rows(proto_ref[own, :])
        gathered(PROTO_RS + h, nx, x_buf.at[h])
        gp_ref[own, :] = project(total_of(x_buf.at[h], nx), unit, inverse).astype(BF16)
        for d in far_first(nx):
            send(PROTO_AG + h, gp_ref.at[own], gp_ref.at[own], at_x(lax.rem(x + d, nx)))
        sent(PROTO_AG + h, gp_ref.at[pl.ds(0, (nx - 1) * xq)])

    def emb_result(h):
        own = pl.ds(c * half + (2 * ai + h) * aq, aq)
        unit, inverse = normalize_rows(emb_ref[own, :])
        gathered(EMB_B + h, ny, b_buf.at[h])
        ge_ref[own, :] = project(total_of(b_buf.at[h], ny), unit, inverse).astype(BF16)
        block = ge_ref.at[own]
        for d in far_first(ny):
            send(EMB_AG + h, block, block, at_a(lax.rem(ai + d, ny)), block_sem.at[h, ai])
        sent(EMB_AG + h, ge_ref.at[pl.ds(0, (ny - 1) * aq)])
        send(TO_SIBLING + h, block, block, sibling)

    for v in range(2):
        for h in range(2):
            slopes(v, h)
    proto_terms(0)
    weight = wcol_ref[pl.ds(pl.multiple_of((1 - c) * half + ai * 2 * aq, 2 * aq), 2 * aq), :]
    total = None
    for offset in range(ny):
        for k in range(2 * tiles):
            at = slice(k * LANES, (k + 1) * LANES)
            ring_slope[offset, :, at] = (ring_soft[offset, :, at] - ring_sink[offset, :, at] * weight).astype(BF16)
        part = jnp.dot(ring_slope[offset], ring_ref[slot(offset)], preferred_element_type=F32)
        total = part if total is None else total + part
    for h in range(2):
        b_buf[h, bi] = total[h * aq : (h + 1) * aq]
        broadcast(EMB_B + h, ny, bi, at_b, b_buf.at[h])
    proto_terms(1)

    cross = row_buf.at[ITERS + 1]
    for v in range(2):
        for i in range(0, half, step):
            here = slice(v * half + i, v * half + i + step)
            s = lax.dot_general(
                eb_ref[here, :], pb_ref[...], (((1,), (1,)), ((), ())), preferred_element_type=F32
            )
            for q in range(0, step, LANES):
                other = slice((1 - v) * half + i + q, (1 - v) * half + i + q + LANES)
                total = None
                for j in range(tiles):
                    part = sink_ref[other, lane[j]] * s[q : q + LANES, lane[j]]
                    total = part if total is None else total + part
                r = (v * half + i + q) // LANES
                cross[pos, r : r + 1, :] = across_lanes(total)
    broadcast(CROSS, 2 * ny, pos, at_yc, cross)

    proto_result(0)
    crossz = rowz_buf.at[ITERS + 1]
    gathered(CROSS, 2 * ny, cross)
    crossz[z] = total_of(cross, 2 * ny)
    broadcast(CROSS + 1, ny, z, at_z, crossz)
    emb_result(0)
    emb_result(1)
    proto_result(1)

    gathered(CROSS + 1, ny, crossz)
    swapped = jnp.concatenate([weights[tiles:], weights[:tiles]], axis=0)
    loss = jnp.log(soft_total) - total_of(crossz, ny) * swapped
    for v in range(2):
        for j in range(tiles):
            loss_ref[v : v + 1, lane[j]] = loss[v * tiles + j : v * tiles + j + 1, :]

    for h in range(2):
        for d in reversed(far_first(ny)):
            j = lax.rem(ai + d, ny)
            block = ge_ref.at[pl.ds(c * half + (2 * j + h) * aq, aq)]
            pltpu.make_async_copy(block, block, block_sem.at[h, j]).wait()
            send(TO_SIBLING + h, block, block, sibling)
        sent(TO_SIBLING + h, ge_ref.at[pl.ds(0, step)])
    for h in range(2):
        arrived(PROTO_AG + h, gp_ref.at[pl.ds(0, (nx - 1) * xq)])
    flush()
    for h in range(2):
        arrived(TO_SIBLING + h, ge_ref.at[pl.ds(0, step)])


def finish(ge_ref, gp_ref, loss_ref, ge_out, gp_out, loss_out, sem):
    copies = [
        pltpu.make_async_copy(ge_ref, ge_out, sem.at[0]),
        pltpu.make_async_copy(gp_ref, gp_out, sem.at[1]),
        pltpu.make_async_copy(loss_ref, loss_out, sem.at[2]),
    ]
    for copy in copies:
        copy.start()
    for copy in copies:
        copy.wait()


def body(nx, ny, embeddings, prototypes):
    views, samples, width = embeddings.shape
    rows, cols = views * samples, prototypes.shape[0]
    aq, xq = samples // 2 // ny, cols // 2 // nx
    vmem = pl.BlockSpec(memory_space=pltpu.VMEM)
    hbm = pl.BlockSpec(memory_space=pltpu.HBM)
    shapes = (
        jax.ShapeDtypeStruct((rows, width), BF16),
        jax.ShapeDtypeStruct((cols, width), BF16),
        jax.ShapeDtypeStruct((views, samples), F32),
    )
    results = pl.pallas_call(
        functools.partial(kernel, nx, ny),
        out_shape=shapes,
        in_specs=[hbm, hbm],
        out_specs=(vmem, vmem, vmem),
        scratch_shapes=[
            pltpu.VMEM((rows, width), BF16),
            pltpu.VMEM((cols, width), BF16),
            pltpu.VMEM((rows, width), BF16),
            pltpu.VMEM((cols, width), BF16),
            pltpu.VMEM((rows, cols), F32),
            pltpu.VMEM((rows, cols), F32),
            pltpu.VMEM((rows, cols), BF16),
            pltpu.VMEM((ny, 2 * cols, width), BF16),
            pltpu.VMEM((ny, 2 * aq, 2 * cols), F32),
            pltpu.VMEM((ny, 2 * aq, 2 * cols), F32),
            pltpu.VMEM((ny, 2 * aq, 2 * cols), BF16),
            pltpu.VMEM((cols, width), F32),
            pltpu.VMEM((rows, LANES), F32),
            pltpu.VMEM((rows, LANES), F32),
            pltpu.VMEM((SUB, LANES), F32),
            pltpu.VMEM((ITERS, nx, SUB, LANES), F32),
            pltpu.VMEM((ITERS + 2, 2 * ny, SUB, LANES), F32),
            pltpu.VMEM((ITERS + 2, ny, SUB, LANES), F32),
            pltpu.VMEM((2 * ny, SUB, LANES), F32),
            pltpu.VMEM((2, ny, aq, width), F32),
            pltpu.VMEM((2, nx, xq, width), F32),
            pltpu.SemaphoreType.DMA((2,)),
            pltpu.SemaphoreType.DMA((STAGES,)),
            pltpu.SemaphoreType.DMA((STAGES,)),
            pltpu.SemaphoreType.DMA((ny,)),
            pltpu.SemaphoreType.DMA((2, ny)),
        ],
        compiler_params=pltpu.CompilerParams(
            collective_id=0, has_side_effects=True, vmem_limit_bytes=48 * 2**20
        ),
    )(
        pltpu.with_memory_space_constraint(embeddings.reshape(rows, width), pltpu.HBM),
        pltpu.with_memory_space_constraint(prototypes, pltpu.HBM),
    )
    ge, gp, loss = pl.pallas_call(
        finish,
        out_shape=shapes,
        in_specs=[vmem, vmem, vmem],
        out_specs=(hbm, hbm, hbm),
        scratch_shapes=[pltpu.SemaphoreType.DMA((3,))],
        compiler_params=pltpu.CompilerParams(vmem_limit_bytes=8 * 2**20),
    )(*results)
    return ge.reshape(views, samples, width), gp, loss


def solution(mesh):
    nx = mesh.shape["samp"]
    ny = 1
    while 2 * ny * ny < mesh.shape["proto"]:
        ny += 1
    return jax.shard_map(
        functools.partial(body, nx, ny),
        mesh=mesh,
        in_specs=(P(None, "samp", None), P("proto", None)),
        out_specs=(P(None, "samp", None), P("proto", None), P(None, "samp")),
        check_vma=False,
    )
```
